32 devices in a mesh: row: 4 (over y, x), col: 8 (over z, core).
Axes of the slice: x: 2, y: 2, z: 4, core: 2. Of those that a mesh axis runs over, the one named last changes fastest.
Arguments:
- teacher_feats: bfloat16 [64, 64, 2048], P(None, 'row', 'col'), may hold values from -6 to 6
- teacher_probs: float32 [8, 64, 2048], P(None, 'row', 'col'), may hold values from 0 to 1, as said below
- student_feats: bfloat16 [256, 64, 2048], P(None, 'row', 'col'), may hold values from 0 to 8
- conv_weight: bfloat16 [9, 256, 256], replicated, may hold values from -0.125 to 0.125
- class_weight: bfloat16 [256, 8], replicated, may hold values from -3 to 3
Outputs:
- refined: float32 [8, 64, 2048], P(None, 'row', 'col')
- feature_grad: bfloat16 [256, 64, 2048], P(None, 'row', 'col')
- grad_conv: float32 [9, 256, 256], replicated
- grad_class: float32 [256, 8], replicated
The draws below stay inside these ranges and needn't reach their ends.
Inputs may be any that keep to these rules, and one draw needn't show every extreme that they name: `teacher_probs`: at every pixel the 8 values are positive and sum to one.
All inputs are finite; a program needn't handle non-finite values.
Results may differ from the reference program's by a relative error of at most 0.002.
The reference program's roundings to bfloat16 on the way (of `hidden`, `error_term` and `back_error`) count: a program that leaves them out, or rounds other values in their place, can miss the bound.
Values may be sent and summed in bfloat16 or wider, within the bound.
A program may use at most 128 MiB of HBM per device.

```python
import jax
import jax.numpy as jnp

TEACHER_CH = 64
STUDENT_CH = 256
HIDDEN_SIZE = 256
CLASSES = 8
ITERS = 4
ROWS_DEV = 16
COLS_DEV = 256
HEIGHT = 64
WIDTH = 2048


def draw_teacher_feats(key, part):
    value_key, scale_key = jax.random.split(jax.random.fold_in(key, 11))
    values = jax.random.truncated_normal(value_key, -4.0, 4.0, (TEACHER_CH, HEIGHT, WIDTH), jnp.float32)
    scales = jnp.exp(jax.random.uniform(scale_key, (1, HEIGHT, WIDTH), jnp.float32, jnp.log(0.3), jnp.log(1.5)))
    return (values * scales).astype(jnp.bfloat16)


def draw_teacher_probs(key, part):
    region_key, pixel_key = jax.random.split(jax.random.fold_in(key, 23))
    blocks = 2.0 * jax.random.normal(region_key, (CLASSES, 2 * HEIGHT // ROWS_DEV, 2 * WIDTH // COLS_DEV), jnp.float32)
    coarse = jnp.repeat(jnp.repeat(blocks, ROWS_DEV // 2, axis=1), COLS_DEV // 2, axis=2)
    logits = coarse + jax.random.normal(pixel_key, (CLASSES, HEIGHT, WIDTH), jnp.float32)
    return jax.nn.softmax(logits, axis=0).astype(jnp.float32)


def draw_student_feats(key, part):
    region_key, pixel_key = jax.random.split(jax.random.fold_in(key, 37))
    low_scale = 0.01
    low_value = 0.0
    block_scale = jnp.exp(jax.random.uniform(region_key, (1, 2 * HEIGHT // ROWS_DEV, 2 * WIDTH // COLS_DEV), jnp.float32, jnp.log(low_scale), jnp.log(10.0)))
    coarse = jnp.repeat(jnp.repeat(block_scale, ROWS_DEV // 2, axis=1), COLS_DEV // 2, axis=2)
    values = jax.random.uniform(pixel_key, (STUDENT_CH, HEIGHT, WIDTH), jnp.float32, low_value, 0.8)
    return (values * coarse).astype(jnp.bfloat16)


def noise(own_key, dims, spread, reach, kind=jnp.bfloat16):
    array = jax.random.normal(own_key, dims, jnp.float32) * spread
    return jnp.minimum(jnp.maximum(array, -reach), reach).astype(kind)


def setup_inputs(seed: int = 0) -> dict:
    streams_of = jax.random.split(jax.random.key(seed), 6)
    return {
        "teacher_feats": draw_teacher_feats(jax.random.fold_in(streams_of[5], 71), 0),
        "teacher_probs": draw_teacher_probs(jax.random.fold_in(streams_of[5], 71), 0),
        "student_feats": draw_student_feats(jax.random.fold_in(streams_of[5], 71), 0),
        "conv_weight": noise(streams_of[3], (9, STUDENT_CH, HIDDEN_SIZE), (9 * STUDENT_CH) ** -0.5, 0.125),
        "class_weight": noise(streams_of[4], (HIDDEN_SIZE, CLASSES), 0.5, 3.0),
    }


def tap_list():
    offsets = [(0, 0)]
    for radius in (1, 2, 4):
        for step_y in (-1, 0, 1):
            for step_x in (-1, 0, 1):
                if step_y != 0 or step_x != 0:
                    offsets.append((step_y * radius, step_x * radius))
    return offsets


def conv_taps():
    return [(off_y, off_x) for off_y in (-1, 0, 1) for off_x in (-1, 0, 1)]


def window(padded, margin, off_y, off_x, rows_here, cols_here):
    return padded[:, margin + off_y:margin + off_y + rows_here, margin + off_x:margin + off_x + cols_here]


def silu_slope(pre_act):
    logistic = jax.nn.sigmoid(pre_act)
    return logistic * (1.0 + pre_act * (1.0 - logistic))


def reference(teacher_feats, teacher_probs, student_feats, conv_weight, class_weight):
    rows_here, cols_here = teacher_probs.shape[1], teacher_probs.shape[2]
    margin = 4
    pad_spec = ((0, 0), (margin, margin), (margin, margin))
    features = jnp.pad(teacher_feats.astype(jnp.float32), pad_spec)
    inside = jnp.pad(jnp.ones((1, rows_here, cols_here), jnp.float32), pad_spec)
    center = window(features, margin, 0, 0, rows_here, cols_here)
    tap_terms = []
    for off_y, off_x in tap_list():
        neighbour = window(features, margin, off_y, off_x, rows_here, cols_here)
        distance = jnp.sum((center - neighbour) ** 2, axis=0)
        present = window(inside, margin, off_y, off_x, rows_here, cols_here)[0]
        tap_terms.append(present * jnp.exp(-distance / teacher_feats.shape[0]))
    stacked = jnp.stack(tap_terms)
    weights = stacked / jnp.sum(stacked, axis=0)
    current = teacher_probs
    for sweep_index in range(ITERS):
        padded = jnp.pad(current, pad_spec)
        running = jnp.zeros(current.shape, jnp.float32)
        for position, (off_y, off_x) in enumerate(tap_list()):
            running = running + weights[position][None] * window(padded, margin, off_y, off_x, rows_here, cols_here)
        current = running
    refined = current

    channels = student_feats.shape[0]
    pixels = rows_here * cols_here
    unit_pad = ((0, 0), (1, 1), (1, 1))
    student_pad = jnp.pad(student_feats, unit_pad)
    pre_act = jnp.zeros((conv_weight.shape[2], pixels), jnp.float32)
    for tap_index, (off_y, off_x) in enumerate(conv_taps()):
        shifted = window(student_pad, 1, off_y, off_x, rows_here, cols_here).reshape(channels, pixels)
        pre_act = pre_act + jnp.dot(conv_weight[tap_index].T, shifted, preferred_element_type=jnp.float32)
    hidden = jax.nn.silu(pre_act).astype(jnp.bfloat16)
    class_logit = jnp.dot(class_weight.T, hidden, preferred_element_type=jnp.float32)
    error_term = (jax.nn.sigmoid(class_logit) - refined.reshape(-1, pixels)).astype(jnp.bfloat16)
    back_sum = jnp.dot(class_weight, error_term, preferred_element_type=jnp.float32)
    back_error = (back_sum * silu_slope(pre_act)).astype(jnp.bfloat16)
    pixel_count = float(ROWS_DEV * COLS_DEV)
    grad_class = jnp.dot(hidden, error_term.T, preferred_element_type=jnp.float32) / pixel_count
    error_pad = jnp.pad(back_error.reshape(-1, rows_here, cols_here), unit_pad)
    conv_grads = []
    feature_sum = jnp.zeros((channels, pixels), jnp.float32)
    for tap_index, (off_y, off_x) in enumerate(conv_taps()):
        shifted = window(student_pad, 1, off_y, off_x, rows_here, cols_here).reshape(channels, pixels)
        conv_grads.append(jnp.dot(shifted, back_error.T, preferred_element_type=jnp.float32) / pixel_count)
        moved = window(error_pad, 1, -off_y, -off_x, rows_here, cols_here).reshape(-1, pixels)
        feature_sum = feature_sum + jnp.dot(conv_weight[tap_index], moved, preferred_element_type=jnp.float32)
    feature_grad = feature_sum.astype(jnp.bfloat16).reshape(channels, rows_here, cols_here)
    return refined, feature_grad, jnp.stack(conv_grads), grad_class
```

```python
import functools

import jax
import jax.numpy as jnp
from jax import lax
from jax.experimental import pallas as pl
from jax.experimental.pallas import tpu as pltpu
from jax.sharding import PartitionSpec as P

ITERS = 4


def with_halo(cells, sides, width):
    for axis, dim in sides:
        count = lax.axis_size(axis)
        ends = count - 1
        head = lax.slice_in_dim(cells, 0, width, axis=dim)
        tail = lax.slice_in_dim(cells, cells.shape[dim] - width, cells.shape[dim], axis=dim)
        cells = jnp.concatenate(
            [
                lax.ppermute(tail, axis, [(i, (i + 1) % count) for i in range(ends)]),
                cells,
                lax.ppermute(head, axis, [((i + 1) % count, i) for i in range(ends)]),
            ],
            axis=dim,
        )
    return cells


def tap_list():
    offsets = [(0, 0)]
    for radius in (1, 2, 4):
        for step_y in (-1, 0, 1):
            for step_x in (-1, 0, 1):
                if step_y != 0 or step_x != 0:
                    offsets.append((step_y * radius, step_x * radius))
    return offsets


def conv_taps():
    return [(off_y, off_x) for off_y in (-1, 0, 1) for off_x in (-1, 0, 1)]


def window(padded, margin, off_y, off_x, rows_here, cols_here):
    return padded[
        :, margin + off_y : margin + off_y + rows_here, margin + off_x : margin + off_x + cols_here
    ]


def silu_slope(pre_act):
    logistic = jax.nn.sigmoid(pre_act)
    return logistic * (1.0 + pre_act * (1.0 - logistic))


def line_inside(start, count, extend, full):
    places = start - extend + jnp.arange(count + 2 * extend, dtype=jnp.int32)
    return ((places >= 0) & (places < full)).astype(jnp.float32)


def affinity_weights(features, inside, extend, rows_here, cols_here):
    margin = 4
    span_y = rows_here + 2 * extend
    span_x = cols_here + 2 * extend
    center = features[:, margin : margin + span_y, margin : margin + span_x].astype(jnp.float32)
    tap_terms = []
    for position, (off_y, off_x) in enumerate(tap_list()):
        if position == 0:
            tap_terms.append(jnp.ones((span_y, span_x), jnp.float32))
        else:
            neighbour = features[
                :,
                margin + off_y : margin + off_y + span_y,
                margin + off_x : margin + off_x + span_x,
            ].astype(jnp.float32)
            distance = jnp.sum((center - neighbour) ** 2, axis=0)
            present = inside[
                margin + off_y : margin + off_y + span_y, margin + off_x : margin + off_x + span_x
            ]
            tap_terms.append(present * jnp.exp(-distance / features.shape[0]))
    stacked = jnp.stack(tap_terms)
    return stacked / jnp.sum(stacked, axis=0)


def propagate(weights, padded, span_y, span_x):
    running = jnp.zeros((padded.shape[0], span_y, span_x), jnp.float32)
    for position, (off_y, off_x) in enumerate(tap_list()):
        running = running + weights[position][None] * window(
            padded, 4, off_y, off_x, span_y, span_x
        )
    return running


def shards(teacher_feats, teacher_probs, student_feats, conv_weight, class_weight):
    rows_here, cols_here = (teacher_probs.shape[1], teacher_probs.shape[2])
    row_start = lax.axis_index("row") * rows_here
    col_start = lax.axis_index("col") * cols_here
    full_rows = rows_here * lax.axis_size("row")
    full_cols = cols_here * lax.axis_size("col")
    deep_rim = 4 * ITERS
    extend = deep_rim - 4
    features = with_halo(teacher_feats, (("row", 1), ("col", 2)), deep_rim)
    current = with_halo(teacher_probs, (("row", 1), ("col", 2)), deep_rim)
    inside = (
        line_inside(row_start, rows_here, deep_rim, full_rows)[:, None]
        * line_inside(col_start, cols_here, deep_rim, full_cols)[None, :]
    )
    weights = affinity_weights(features, inside, extend, rows_here, cols_here)
    for sweep_index in range(ITERS):
        inner_rim = deep_rim - 4 * (sweep_index + 1)
        start_at = extend - inner_rim
        span_y = rows_here + 2 * inner_rim
        span_x = cols_here + 2 * inner_rim
        weights_now = weights[:, start_at : start_at + span_y, start_at : start_at + span_x]
        current = propagate(weights_now, current, span_y, span_x)
    channels = student_feats.shape[0]
    pixels = rows_here * cols_here
    pixel_count = float(rows_here * cols_here)
    student_pad = with_halo(student_feats, (("row", 1), ("col", 2)), 1)
    pre_act = jnp.zeros((conv_weight.shape[2], pixels), jnp.float32)
    for tap_index, (off_y, off_x) in enumerate(conv_taps()):
        shifted = window(student_pad, 1, off_y, off_x, rows_here, cols_here).reshape(
            channels, pixels
        )
        pre_act = pre_act + jnp.einsum(
            "ch,cp->hp", conv_weight[tap_index], shifted, preferred_element_type=jnp.float32
        )
    hidden = jax.nn.silu(pre_act).astype(jnp.bfloat16)
    class_logit = jnp.einsum("hk,hp->kp", class_weight, hidden, preferred_element_type=jnp.float32)
    error_term = (jax.nn.sigmoid(class_logit) - current.reshape(-1, pixels)).astype(jnp.bfloat16)
    back_sum = jnp.einsum("hk,kp->hp", class_weight, error_term, preferred_element_type=jnp.float32)
    back_error = (back_sum * silu_slope(pre_act)).astype(jnp.bfloat16)
    class_part = jnp.einsum("hp,kp->hk", hidden, error_term, preferred_element_type=jnp.float32)
    error_pad = with_halo(back_error.reshape(-1, rows_here, cols_here), (("row", 1), ("col", 2)), 1)
    conv_parts = []
    feature_sum = jnp.zeros((channels, pixels), jnp.float32)
    for tap_index, (off_y, off_x) in enumerate(conv_taps()):
        shifted = window(student_pad, 1, off_y, off_x, rows_here, cols_here).reshape(
            channels, pixels
        )
        tap_part = jnp.einsum("cp,hp->ch", shifted, back_error, preferred_element_type=jnp.float32)
        conv_parts.append(tap_part)
        moved = window(error_pad, 1, -off_y, -off_x, rows_here, cols_here).reshape(-1, pixels)
        feature_sum = feature_sum + jnp.einsum(
            "ch,hp->cp", conv_weight[tap_index], moved, preferred_element_type=jnp.float32
        )
    feature_grad = feature_sum.astype(jnp.bfloat16).reshape(channels, rows_here, cols_here)
    taps, _, width = conv_weight.shape
    grad_conv, grad_class = reduce_all(
        jnp.concatenate(conv_parts, axis=0), class_part.T, 1.0 / pixel_count
    )
    grad_conv = grad_conv.reshape(taps, channels, width)
    grad_class = grad_class.T
    return (current, feature_grad, grad_conv, grad_class)


MESH = pl.DeviceIdType.MESH


def remote(src, dst, sems, slot, row, col):
    return pltpu.make_async_remote_copy(
        src_ref=src,
        dst_ref=dst,
        send_sem=sems.at[0, slot],
        recv_sem=sems.at[1, slot],
        device_id=(row, col),
        device_id_type=MESH,
    )


def finish(copies):
    for copy in copies:
        copy.wait()


def reduce_body(nr, nz, scale, g_ref, cls_ref, out_ref, outc_ref, core_buf, row_buf, z_buf, fin, cls_core, cls_row, cls_z, sems):
    row = lax.axis_index("row")
    col = lax.axis_index("col")
    core = lax.rem(col, 2)
    z = col // 2
    twin = z * 2 + 1 - core
    total = g_ref.shape[0]
    part = total // nr
    piece = part // nz
    mine = pl.ds(pl.multiple_of(core * 128, 128), 128)
    other = pl.ds(pl.multiple_of((1 - core) * 128, 128), 128)
    slot = 0
    copies = [
        remote(g_ref.at[:, other], core_buf, sems, 0, row, twin),
        remote(cls_ref, cls_core, sems, 1, row, twin),
    ]
    for copy in copies:
        copy.start()
    finish(copies)
    slot = 2
    core_buf[...] = core_buf[...] + g_ref[:, mine]
    cls_row[row] = cls_ref[...] + cls_core[...]
    copies = []
    for step in range(1, nr):
        to = lax.rem(row + step, nr)
        copies.append(
            remote(core_buf.at[pl.ds(pl.multiple_of(to * part, 16), part)], row_buf.at[step - 1], sems, slot, to, col)
        )
        copies.append(remote(cls_row.at[row], cls_row.at[row], sems, slot + 1, to, col))
        slot += 2
    for copy in copies:
        copy.start()
    finish(copies)
    kept = pl.ds(pl.multiple_of(row * part, 16), part)
    summed = core_buf[kept]
    for step in range(1, nr):
        summed = summed + row_buf[step - 1]
    row_buf[0] = summed
    across = cls_row[0]
    for i in range(1, nr):
        across = across + cls_row[i]
    cls_z[z] = across
    copies = []
    for step in range(1, nz):
        to = lax.rem(z + step, nz)
        copies.append(
            remote(row_buf.at[0, pl.ds(pl.multiple_of(to * piece, 16), piece)], z_buf.at[step - 1], sems, slot, row, to * 2 + core)
        )
        copies.append(remote(cls_z.at[z], cls_z.at[z], sems, slot + 1, row, to * 2 + core))
        slot += 2
    for copy in copies:
        copy.start()
    finish(copies)
    summed = row_buf[0, pl.ds(pl.multiple_of(z * piece, 16), piece)]
    for step in range(1, nz):
        summed = summed + z_buf[step - 1]
    own = pl.ds(pl.multiple_of(row * part + z * piece, 16), piece)
    fin[core, own] = (summed * scale).astype(jnp.bfloat16)
    across = cls_z[0]
    for i in range(1, nz):
        across = across + cls_z[i]
    outc_ref[...] = across * scale
    copies = []
    for step in range(1, nz):
        to = lax.rem(z + step, nz)
        copies.append(remote(fin.at[core, own], fin.at[core, own], sems, slot, row, to * 2 + core))
        slot += 1
    for copy in copies:
        copy.start()
    finish(copies)
    copies = []
    for step in range(1, nr):
        to = lax.rem(row + step, nr)
        copies.append(remote(fin.at[core, kept], fin.at[core, kept], sems, slot, to, col))
        slot += 1
    for copy in copies:
        copy.start()
    finish(copies)
    copy = remote(fin.at[core], fin.at[core], sems, slot, row, twin)
    copy.start()
    copy.wait()
    out_ref[:, :128] = fin[0].astype(jnp.float32)
    out_ref[:, 128:] = fin[1].astype(jnp.float32)


def reduce_barrier(nr, nz):
    row = lax.axis_index("row")
    col = lax.axis_index("col")
    core = lax.rem(col, 2)
    z = col // 2
    barrier = pltpu.get_barrier_semaphore()
    pl.semaphore_signal(barrier, inc=1, device_id=(row, z * 2 + 1 - core), device_id_type=MESH)
    for step in range(1, nr):
        pl.semaphore_signal(barrier, inc=1, device_id=(lax.rem(row + step, nr), col), device_id_type=MESH)
    for step in range(1, nz):
        pl.semaphore_signal(barrier, inc=1, device_id=(row, lax.rem(z + step, nz) * 2 + core), device_id_type=MESH)
    pl.semaphore_wait(barrier, nr + nz - 1)


def reduce_kernel(nr, nz, scale, *refs):
    reduce_barrier(nr, nz)
    reduce_body(nr, nz, scale, *refs)


def reduce_scratch(nr, nz, total, classes, hidden):
    part = total // nr
    return [
        pltpu.VMEM((total, 128), jnp.float32),
        pltpu.VMEM((nr - 1, part, 128), jnp.float32),
        pltpu.VMEM((nz - 1, part // nz, 128), jnp.float32),
        pltpu.VMEM((2, total, 128), jnp.bfloat16),
        pltpu.VMEM((classes, hidden), jnp.float32),
        pltpu.VMEM((nr, classes, hidden), jnp.float32),
        pltpu.VMEM((nz, classes, hidden), jnp.float32),
        pltpu.SemaphoreType.DMA((2, 3 + 3 * (nr - 1) + 3 * (nz - 1))),
    ]


def reduce_all(conv, cls, scale):
    nr = lax.axis_size("row")
    nz = lax.axis_size("col") // 2
    unit = nr * nz * 16
    rows = conv.shape[0]
    total = -(-rows // unit) * unit
    if total > rows:
        conv = jnp.pad(conv, ((0, total - rows), (0, 0)))
    out = pl.pallas_call(
        functools.partial(reduce_kernel, nr, nz, scale),
        out_shape=(jax.ShapeDtypeStruct(conv.shape, jnp.float32), jax.ShapeDtypeStruct(cls.shape, jnp.float32)),
        in_specs=[pl.BlockSpec(memory_space=pltpu.VMEM)] * 2,
        out_specs=[pl.BlockSpec(memory_space=pltpu.VMEM)] * 2,
        scratch_shapes=reduce_scratch(nr, nz, total, *cls.shape),
        compiler_params=pltpu.CompilerParams(collective_id=0, has_side_effects=True, vmem_limit_bytes=40 * 2**20),
    )(conv, cls)
    return out[0][:rows], out[1]


def solution(mesh):
    in_specs = (P(None, "row", "col"), P(None, "row", "col"), P(None, "row", "col"), P(), P())
    out_specs = (P(None, "row", "col"), P(None, "row", "col"), P(), P())
    return jax.shard_map(shards, mesh=mesh, in_specs=in_specs, out_specs=out_specs, check_vma=False)
```

```python
import functools

import jax
import jax.numpy as jnp
from jax import lax
from jax.experimental import pallas as pl
from jax.experimental.pallas import tpu as pltpu
from jax.sharding import PartitionSpec as P

ITERS = 4
REACH = 4
SHIFTS = (0, 1, 2, 4, -1, -2, -4)
SIDES = ((-1, 0), (1, 0), (0, -1), (0, 1), (-1, -1), (-1, 1), (1, -1), (1, 1))


def tap_list():
    offsets = []
    for radius in (1, 2, 4):
        for step_y in (-1, 0, 1):
            for step_x in (-1, 0, 1):
                if step_y != 0 or step_x != 0:
                    offsets.append((step_y * radius, step_x * radius))
    return offsets


MESH = pl.DeviceIdType.MESH


def remote(src, dst, sems, slot, row, col):
    return pltpu.make_async_remote_copy(
        src_ref=src,
        dst_ref=dst,
        send_sem=sems.at[0, slot],
        recv_sem=sems.at[1, slot],
        device_id=(row, col),
        device_id_type=MESH,
    )


def finish(copies):
    for copy in copies:
        copy.wait()


def reduce_body(nr, nz, scale, g_ref, cls_ref, out_ref, outc_ref, core_buf, row_buf, z_buf, fin, cls_core, cls_row, cls_z, sems):
    row = lax.axis_index("row")
    col = lax.axis_index("col")
    core = lax.rem(col, 2)
    z = col // 2
    twin = z * 2 + 1 - core
    total = g_ref.shape[0]
    part = total // nr
    piece = part // nz
    mine = pl.ds(pl.multiple_of(core * 128, 128), 128)
    other = pl.ds(pl.multiple_of((1 - core) * 128, 128), 128)
    slot = 0
    copies = [
        remote(g_ref.at[:, other], core_buf, sems, 0, row, twin),
        remote(cls_ref, cls_core, sems, 1, row, twin),
    ]
    for copy in copies:
        copy.start()
    yield
    finish(copies)
    slot = 2
    core_buf[...] = core_buf[...] + g_ref[:, mine]
    cls_row[row] = cls_ref[...] + cls_core[...]
    copies = []
    for step in range(1, nr):
        to = lax.rem(row + step, nr)
        copies.append(
            remote(core_buf.at[pl.ds(pl.multiple_of(to * part, 16), part)], row_buf.at[step - 1], sems, slot, to, col)
        )
        copies.append(remote(cls_row.at[row], cls_row.at[row], sems, slot + 1, to, col))
        slot += 2
    for copy in copies:
        copy.start()
    yield
    finish(copies)
    kept = pl.ds(pl.multiple_of(row * part, 16), part)
    summed = core_buf[kept]
    for step in range(1, nr):
        summed = summed + row_buf[step - 1]
    row_buf[0] = summed
    across = cls_row[0]
    for i in range(1, nr):
        across = across + cls_row[i]
    cls_z[z] = across
    copies = []
    for step in range(1, nz):
        to = lax.rem(z + step, nz)
        copies.append(
            remote(row_buf.at[0, pl.ds(pl.multiple_of(to * piece, 16), piece)], z_buf.at[step - 1], sems, slot, row, to * 2 + core)
        )
        copies.append(remote(cls_z.at[z], cls_z.at[z], sems, slot + 1, row, to * 2 + core))
        slot += 2
    for copy in copies:
        copy.start()
    yield
    finish(copies)
    summed = row_buf[0, pl.ds(pl.multiple_of(z * piece, 16), piece)]
    for step in range(1, nz):
        summed = summed + z_buf[step - 1]
    own = pl.ds(pl.multiple_of(row * part + z * piece, 16), piece)
    fin[core, own] = (summed * scale).astype(jnp.bfloat16)
    across = cls_z[0]
    for i in range(1, nz):
        across = across + cls_z[i]
    outc_ref[...] = across * scale
    copies = []
    for step in range(1, nz):
        to = lax.rem(z + step, nz)
        copies.append(remote(fin.at[core, own], fin.at[core, own], sems, slot, row, to * 2 + core))
        slot += 1
    for copy in copies:
        copy.start()
    yield
    finish(copies)
    copies = []
    for step in range(1, nr):
        to = lax.rem(row + step, nr)
        copies.append(remote(fin.at[core, kept], fin.at[core, kept], sems, slot, to, col))
        slot += 1
    for copy in copies:
        copy.start()
    yield
    finish(copies)
    copy = remote(fin.at[core], fin.at[core], sems, slot, row, twin)
    copy.start()
    yield
    copy.wait()
    out_ref[:, :128] = fin[0].astype(jnp.float32)
    out_ref[:, 128:] = fin[1].astype(jnp.float32)


def reduce_scratch(nr, nz, total, classes, hidden):
    part = total // nr
    return [
        pltpu.VMEM((total, 128), jnp.float32),
        pltpu.VMEM((nr - 1, part, 128), jnp.float32),
        pltpu.VMEM((nz - 1, part // nz, 128), jnp.float32),
        pltpu.VMEM((2, total, 128), jnp.bfloat16),
        pltpu.VMEM((classes, hidden), jnp.float32),
        pltpu.VMEM((nr, classes, hidden), jnp.float32),
        pltpu.VMEM((nz, classes, hidden), jnp.float32),
        pltpu.SemaphoreType.DMA((2, 3 + 3 * (nr - 1) + 3 * (nz - 1))),
    ]


def present(down, right):
    row = lax.axis_index("row") + down
    col = lax.axis_index("col") + right
    rows = lax.axis_size("row")
    cols = lax.axis_size("col")
    return (row >= 0) & (row < rows) & (col >= 0) & (col < cols)


def greet_sides(barrier):
    row = lax.axis_index("row")
    col = lax.axis_index("col")
    for down, right in SIDES:

        @pl.when(present(down, right))
        def _():
            pl.semaphore_signal(barrier, inc=1, device_id=(row + down, col + right), device_id_type=MESH)


def count_sides():
    count = 0
    for down, right in SIDES:
        count = count + jnp.where(present(down, right), 1, 0)
    return count


def side_copies(cells, packs, rim_rows, rim_packs, sems, base, span):
    row = lax.axis_index("row")
    col = lax.axis_index("col")
    pixels = cells.shape[1]
    copies = []
    for index, (down, right) in enumerate(SIDES):
        if right == 0:
            source = cells.at[:, pl.ds(0 if down < 0 else pixels - span, span)]
            target = rim_rows.at[index]
        else:
            source = packs.at[0 if right < 0 else 1]
            target = rim_packs.at[index - 2]
        copies.append((down, right, remote(source, target, sems, base + index, row + down, col + right)))
    return copies


def start_sides(copies):
    for down, right, copy in copies:

        @pl.when(present(down, right))
        def _():
            copy.start()


def finish_sides(copies):
    for down, right, copy in copies:

        @pl.when(present(down, right))
        def _():
            copy.wait_send()

        @pl.when(present(-down, -right))
        def _():
            copy.wait_recv()


def clear_sides(rim_rows, rim_packs):
    for index, (down, right) in enumerate(SIDES):

        @pl.when(jnp.logical_not(present(-down, -right)))
        def _():
            if right == 0:
                rim_rows[index] = jnp.zeros(rim_rows.shape[1:], rim_rows.dtype)
            else:
                rim_packs[index - 2] = jnp.zeros(rim_packs.shape[1:], rim_packs.dtype)


def row_at(index, width):
    return pl.ds(pl.multiple_of(index * width, 128), width)


def pack_sides(cells, packs, rows, width, reach):
    lane = lax.broadcasted_iota(jnp.int32, (cells.shape[0], 128), 1)
    zero = jnp.zeros((cells.shape[0], 128), jnp.float32)

    def step(y, held):
        left = cells[:, pl.ds(pl.multiple_of(y * width, 128), 128)].astype(jnp.float32)
        right = cells[:, pl.ds(pl.multiple_of(y * width + width - 128, 128), 128)].astype(jnp.float32)
        here = (lane >= reach * y) & (lane < reach * y + reach)
        return (
            jnp.where(here, pltpu.roll(left, reach * y, 1), held[0]),
            jnp.where(here, pltpu.roll(right, lax.rem(reach * y + reach, 128), 1), held[1]),
        )

    held = lax.fori_loop(0, rows, step, (zero, zero))
    packs[0] = held[0].astype(packs.dtype)
    packs[1] = held[1].astype(packs.dtype)


def rim_tile(pack_left, pack_right, y, reach):
    lane = lax.broadcasted_iota(jnp.int32, pack_left.shape, 1)
    right = pltpu.roll(pack_right.astype(jnp.float32), lax.rem(128 - reach * y, 128), 1)
    left = pltpu.roll(pack_left.astype(jnp.float32), lax.rem(256 - reach - reach * y, 128), 1)
    return jnp.where(lane < reach, right, jnp.where(lane >= 128 - reach, left, 0.0))


def spread(cells, rim_rows, rim_packs, rows, width, reach, emit):
    def top(r, carry):
        tile = rim_tile(rim_packs[5], rim_packs[4], rows - reach + r, reach)
        wide = jnp.concatenate([rim_rows[1, :, row_at(r, width)].astype(jnp.float32), tile], axis=1)
        emit(r, wide)
        return carry

    def centre(r, carry):
        tile = rim_tile(rim_packs[1], rim_packs[0], r, reach)
        wide = jnp.concatenate([cells[:, row_at(r, width)].astype(jnp.float32), tile], axis=1)
        emit(r + reach, wide)
        return carry

    def bottom(r, carry):
        tile = rim_tile(rim_packs[3], rim_packs[2], r, reach)
        wide = jnp.concatenate([rim_rows[0, :, row_at(r, width)].astype(jnp.float32), tile], axis=1)
        emit(r + rows + reach, wide)
        return carry

    lax.fori_loop(0, reach, top, 0)
    lax.fori_loop(0, rows, centre, 0)
    lax.fori_loop(0, reach, bottom, 0)


def teacher_kernel(
    rows, width, feats, probs, refined, moved, weights, sweeps, moved_now, feat_packs, feat_rows, feat_rims,
    packs, prob_rows, prob_rims, sems,
):
    channels = feats.shape[0]
    span = REACH * width
    full_rows = rows * lax.axis_size("row")
    full_cols = width * lax.axis_size("col")
    first_row = lax.axis_index("row") * rows
    first_col = lax.axis_index("col") * width
    clear_sides(feat_rows, feat_rims)
    for sweep in range(ITERS):
        clear_sides(prob_rows.at[sweep], prob_rims.at[sweep])
    pack_sides(feats, feat_packs, rows, width, REACH)
    pack_sides(probs, packs.at[0], rows, width, REACH)
    barrier = pltpu.get_barrier_semaphore()
    greet_sides(barrier)
    pl.semaphore_wait(barrier, count_sides())
    feat_copies = side_copies(feats, feat_packs, feat_rows, feat_rims, sems, 0, span)
    start_sides(feat_copies)
    copies = side_copies(probs, packs.at[0], prob_rows.at[0], prob_rims.at[0], sems, 8, span)
    start_sides(copies)
    finish_sides(feat_copies)

    def emit_feats(r, wide):
        for index, shift in enumerate(SHIFTS):
            turned = wide if shift == 0 else pltpu.roll(wide, (-shift) % wide.shape[1], 1)
            moved[index, :, row_at(r, width)] = turned[:, :width]

    spread(feats, feat_rows, feat_rims, rows, width, REACH, emit_feats)
    place = first_col + lax.broadcasted_iota(jnp.int32, (8, width), 1)

    def weigh(y, carry):
        centre = moved[0, :, row_at(y + REACH, width)]
        total = jnp.ones((8, width), jnp.float32)
        terms = []
        for off_y, off_x in tap_list():
            other = moved[SHIFTS.index(off_x), :, row_at(y + REACH + off_y, width)]
            apart = (centre - other) * (centre - other)
            apart = jnp.sum(apart.reshape(channels // 8, 8, width), axis=0)
            apart = jnp.broadcast_to(jnp.sum(apart, axis=0, keepdims=True), (8, width))
            at_row = first_row + y + off_y
            inside = (place + off_x >= 0) & (place + off_x < full_cols) & (at_row >= 0) & (at_row < full_rows)
            term = jnp.where(inside, jnp.exp(apart * (-1.0 / channels)), 0.0)
            terms.append(term)
            total = total + term
        scale = 1.0 / total
        weights[0, :, row_at(y, width)] = scale
        for index, term in enumerate(terms):
            weights[index + 1, :, row_at(y, width)] = term * scale
        return carry

    lax.fori_loop(0, rows, weigh, 0)

    def emit_probs(r, wide):
        for index, shift in enumerate(SHIFTS):
            turned = wide if shift == 0 else pltpu.roll(wide, (-shift) % wide.shape[1], 1)
            moved_now[index, :, row_at(r, width)] = turned[:, :width]

    for sweep in range(ITERS):
        now = probs if sweep == 0 else sweeps.at[sweep - 1]
        later = refined if sweep == ITERS - 1 else sweeps.at[sweep]
        finish_sides(copies)
        spread(now, prob_rows.at[sweep], prob_rims.at[sweep], rows, width, REACH, emit_probs)

        def gather(y, carry):
            running = weights[0, :, row_at(y, width)] * moved_now[0, :, row_at(y + REACH, width)]
            for index, (off_y, off_x) in enumerate(tap_list()):
                running = running + (
                    weights[index + 1, :, row_at(y, width)]
                    * moved_now[SHIFTS.index(off_x), :, row_at(y + REACH + off_y, width)]
                )
            later[:, row_at(y, width)] = running
            return carry

        lax.fori_loop(0, rows, gather, 0)
        if sweep < ITERS - 1:
            pack_sides(later, packs.at[sweep + 1], rows, width, REACH)
            copies = side_copies(
                later, packs.at[sweep + 1], prob_rows.at[sweep + 1], prob_rims.at[sweep + 1], sems, 16 + 8 * sweep, span
            )
            start_sides(copies)


def refine(feats, probs, rows, width):
    channels, pixels = feats.shape
    classes = probs.shape[0]
    span = REACH * width
    wide = (rows + 2 * REACH) * width
    return pl.pallas_call(
        functools.partial(teacher_kernel, rows, width),
        out_shape=jax.ShapeDtypeStruct(probs.shape, jnp.float32),
        in_specs=[pl.BlockSpec(memory_space=pltpu.VMEM)] * 2,
        out_specs=pl.BlockSpec(memory_space=pltpu.VMEM),
        scratch_shapes=[
            pltpu.VMEM((len(SHIFTS), channels, wide), jnp.float32),
            pltpu.VMEM((25, 8, pixels), jnp.float32),
            pltpu.VMEM((ITERS - 1, classes, pixels), jnp.float32),
            pltpu.VMEM((len(SHIFTS), classes, wide), jnp.float32),
            pltpu.VMEM((2, channels, 128), jnp.bfloat16),
            pltpu.VMEM((2, channels, span), jnp.bfloat16),
            pltpu.VMEM((6, channels, 128), jnp.bfloat16),
            pltpu.VMEM((ITERS, 2, classes, 128), jnp.float32),
            pltpu.VMEM((ITERS, 2, classes, span), jnp.float32),
            pltpu.VMEM((ITERS, 6, classes, 128), jnp.float32),
            pltpu.SemaphoreType.DMA((2, 8 + 8 * ITERS)),
        ],
        compiler_params=pltpu.CompilerParams(collective_id=1, has_side_effects=True, vmem_limit_bytes=48 * 2**20),
    )(feats, probs)


def student_kernel(
    nr, nz, rows, width, scale, cells, ahead, back, class_in, class_out, refined,
    slope_grad, conv_out, class_grad,
    stacked, error, error_turned, error_stacked, parts, class_part,
    cell_packs, cell_rows, cell_rims, error_packs, error_rows, error_rims, side_sems, *reduce_refs,
):
    row = lax.axis_index("row")
    col = lax.axis_index("col")
    core = lax.rem(col, 2)
    z = col // 2
    channels, pixels = cells.shape
    clear_sides(cell_rows, cell_rims)
    clear_sides(error_rows, error_rims)
    pack_sides(cells, cell_packs, rows, width, 1)
    barrier = pltpu.get_barrier_semaphore()
    greet_sides(barrier)
    pl.semaphore_signal(barrier, inc=1, device_id=(row, z * 2 + 1 - core), device_id_type=MESH)
    for step in range(1, nr):
        pl.semaphore_signal(barrier, inc=1, device_id=(lax.rem(row + step, nr), col), device_id_type=MESH)
    for step in range(1, nz):
        pl.semaphore_signal(barrier, inc=1, device_id=(row, lax.rem(z + step, nz) * 2 + core), device_id_type=MESH)
    pl.semaphore_wait(barrier, count_sides() + (nr + nz - 1))
    copies = side_copies(cells, cell_packs, cell_rows, cell_rims, side_sems, 0, width)
    start_sides(copies)
    finish_sides(copies)

    def stack_into(target):
        depth = target.shape[0] // 3

        def emit(r, wide):
            for index, shift in enumerate((-1, 0, 1)):
                turned = wide if shift == 0 else pltpu.roll(wide, (-shift) % wide.shape[1], 1)
                target[index * depth : (index + 1) * depth, row_at(r, width)] = turned[:, :width].astype(target.dtype)

        return emit

    spread(cells, cell_rows, cell_rims, rows, width, 1, stack_into(stacked))
    class_part[...] = jnp.zeros_like(class_part)

    def forward(y, carry):
        here = row_at(y, width)
        pre = jnp.dot(ahead[0], stacked[:, here], preferred_element_type=jnp.float32)
        for tap_row in (1, 2):
            pre = pre + jnp.dot(
                ahead[tap_row], stacked[:, row_at(y + tap_row, width)], preferred_element_type=jnp.float32
            )
        gate = jax.nn.sigmoid(pre)
        hidden = (pre * gate).astype(jnp.bfloat16)
        logit = jnp.dot(class_in[...], hidden, preferred_element_type=jnp.float32)
        wrong = (jax.nn.sigmoid(logit) - refined[:, here]).astype(jnp.bfloat16)
        pull = jnp.dot(class_out[...], wrong, preferred_element_type=jnp.float32)
        slope = pull * (gate * (1.0 + pre * (1.0 - gate)))
        error[:, here] = slope.astype(jnp.bfloat16)
        error_turned[here, :] = slope.T.astype(jnp.bfloat16)
        class_part[...] += lax.dot_general(
            wrong, hidden, (((1,), (1,)), ((), ())), preferred_element_type=jnp.float32
        )
        return carry

    lax.fori_loop(0, rows, forward, 0)
    pack_sides(error, error_packs, rows, width, 1)
    copies = side_copies(error, error_packs, error_rows, error_rims, side_sems, 8, width)
    start_sides(copies)
    depth = stacked.shape[0]
    for tap_row in range(3):
        for index in range(3):
            block = pl.ds(index * channels, channels)
            parts[tap_row * depth + index * channels : tap_row * depth + (index + 1) * channels, :] = jnp.dot(
                stacked[block, tap_row * width : tap_row * width + pixels],
                error_turned[...],
                preferred_element_type=jnp.float32,
            )
    if parts.shape[0] > 3 * depth:
        parts[3 * depth :, :] = jnp.zeros((parts.shape[0] - 3 * depth, parts.shape[1]), jnp.float32)

    def features(y, carry):
        total = jnp.dot(back[0], error_stacked[:, row_at(y, width)], preferred_element_type=jnp.float32)
        for tap_row in (1, 2):
            total = total + jnp.dot(
                back[tap_row], error_stacked[:, row_at(y + tap_row, width)], preferred_element_type=jnp.float32
            )
        slope_grad[:, row_at(y, width)] = total.astype(jnp.bfloat16)
        return carry

    phases = reduce_body(nr, nz, scale, parts, class_part, conv_out, class_grad, *reduce_refs)
    for phase, _ in enumerate(phases):
        if phase == 0:
            finish_sides(copies)
        elif phase == 1:
            spread(error, error_rows, error_rims, rows, width, 1, stack_into(error_stacked))
            lax.fori_loop(0, rows, features, 0)


def student(cells, conv_weight, class_weight, refined, rows, width):
    channels, pixels = cells.shape
    hidden, classes = class_weight.shape
    nr = lax.axis_size("row")
    nz = lax.axis_size("col") // 2
    unit = nr * nz * 16
    wide = (rows + 2) * width
    total = -(-9 * channels // unit) * unit
    taps = conv_weight.reshape(3, 3, channels, hidden)
    ahead = taps.transpose(0, 3, 1, 2).reshape(3, hidden, 3 * channels)
    back = taps[::-1, ::-1].transpose(0, 2, 1, 3).reshape(3, channels, 3 * hidden)
    out = pl.pallas_call(
        functools.partial(student_kernel, nr, nz, rows, width, 1.0 / pixels),
        out_shape=(
            jax.ShapeDtypeStruct((channels, pixels), jnp.bfloat16),
            jax.ShapeDtypeStruct((total, hidden), jnp.float32),
            jax.ShapeDtypeStruct((classes, hidden), jnp.float32),
        ),
        in_specs=[pl.BlockSpec(memory_space=pltpu.VMEM)] * 6,
        out_specs=[pl.BlockSpec(memory_space=pltpu.VMEM)] * 3,
        scratch_shapes=[
            pltpu.VMEM((3 * channels, wide), jnp.bfloat16),
            pltpu.VMEM((hidden, pixels), jnp.bfloat16),
            pltpu.VMEM((pixels, hidden), jnp.bfloat16),
            pltpu.VMEM((3 * hidden, wide), jnp.bfloat16),
            pltpu.VMEM((total, hidden), jnp.float32),
            pltpu.VMEM((classes, hidden), jnp.float32),
            pltpu.VMEM((2, channels, 128), jnp.bfloat16),
            pltpu.VMEM((2, channels, width), jnp.bfloat16),
            pltpu.VMEM((6, channels, 128), jnp.bfloat16),
            pltpu.VMEM((2, hidden, 128), jnp.bfloat16),
            pltpu.VMEM((2, hidden, width), jnp.bfloat16),
            pltpu.VMEM((6, hidden, 128), jnp.bfloat16),
            pltpu.SemaphoreType.DMA((2, 16)),
        ]
        + reduce_scratch(nr, nz, total, classes, hidden),
        compiler_params=pltpu.CompilerParams(collective_id=0, has_side_effects=True, vmem_limit_bytes=56 * 2**20),
    )(cells, ahead, back, class_weight.T, class_weight, refined)
    return out[0], out[1][: 9 * channels], out[2]


def shards(teacher_feats, teacher_probs, student_feats, conv_weight, class_weight):
    classes, rows, width = teacher_probs.shape
    channels = student_feats.shape[0]
    pixels = rows * width
    refined = refine(
        teacher_feats.reshape(teacher_feats.shape[0], pixels), teacher_probs.reshape(classes, pixels), rows, width
    )
    feature_grad, grad_conv, grad_class = student(
        student_feats.reshape(channels, pixels), conv_weight, class_weight, refined, rows, width
    )
    return (
        refined.reshape(classes, rows, width),
        feature_grad.reshape(channels, rows, width),
        grad_conv.reshape(conv_weight.shape),
        grad_class.T,
    )


def solution(mesh):
    in_specs = (P(None, "row", "col"), P(None, "row", "col"), P(None, "row", "col"), P(), P())
    out_specs = (P(None, "row", "col"), P(None, "row", "col"), P(), P())
    return jax.shard_map(shards, mesh=mesh, in_specs=in_specs, out_specs=out_specs, check_vma=False)
```

```python
import functools

import jax
import jax.numpy as jnp
from jax import lax
from jax.experimental import pallas as pl
from jax.experimental.pallas import tpu as pltpu
from jax.sharding import PartitionSpec as P

ITERS = 4
REACH = 4
SHIFTS = (0, 1, 2, 4, -1, -2, -4)
SIDES = ((-1, 0), (1, 0), (0, -1), (0, 1), (-1, -1), (-1, 1), (1, -1), (1, 1))


def tap_list():
    offsets = []
    for radius in (1, 2, 4):
        for step_y in (-1, 0, 1):
            for step_x in (-1, 0, 1):
                if step_y != 0 or step_x != 0:
                    offsets.append((step_y * radius, step_x * radius))
    return offsets


MESH = pl.DeviceIdType.MESH


def remote(src, dst, sems, slot, row, col):
    return pltpu.make_async_remote_copy(
        src_ref=src,
        dst_ref=dst,
        send_sem=sems.at[0, slot],
        recv_sem=sems.at[1, slot],
        device_id=(row, col),
        device_id_type=MESH,
    )


def finish(copies):
    for copy in copies:
        copy.wait()


def reduce_body(nr, nz, scale, g_ref, out_ref, core_buf, row_buf, z_buf, fin, sems, extra=None):
    if extra is not None:
        cls_ref, outc_ref, cls_core, cls_row, cls_z = extra
    row = lax.axis_index("row")
    col = lax.axis_index("col")
    core = lax.rem(col, 2)
    z = col // 2
    twin = z * 2 + 1 - core
    total = g_ref.shape[0]
    part = total // nr
    piece = part // nz
    mine = pl.ds(pl.multiple_of(core * 128, 128), 128)
    other = pl.ds(pl.multiple_of((1 - core) * 128, 128), 128)
    slot = 0
    copies = [remote(g_ref.at[:, other], core_buf, sems, 0, row, twin)]
    if extra is not None:
        copies.append(remote(cls_ref, cls_core, sems, 1, row, twin))
    for copy in copies:
        copy.start()
    yield
    finish(copies)
    slot = 2
    core_buf[...] = core_buf[...] + g_ref[:, mine]
    if extra is not None:
        cls_row[row] = cls_ref[...] + cls_core[...]
    copies = []
    for step in range(1, nr):
        to = lax.rem(row + step, nr)
        copies.append(
            remote(core_buf.at[pl.ds(pl.multiple_of(to * part, 16), part)], row_buf.at[step - 1], sems, slot, to, col)
        )
        if extra is not None:
            copies.append(remote(cls_row.at[row], cls_row.at[row], sems, slot + 1, to, col))
        slot += 2
    for copy in copies:
        copy.start()
    yield
    finish(copies)
    kept = pl.ds(pl.multiple_of(row * part, 16), part)
    summed = core_buf[kept]
    for step in range(1, nr):
        summed = summed + row_buf[step - 1]
    row_buf[0] = summed
    if extra is not None:
        across = cls_row[0]
        for i in range(1, nr):
            across = across + cls_row[i]
        cls_z[z] = across
    copies = []
    for step in range(1, nz):
        to = lax.rem(z + step, nz)
        copies.append(
            remote(row_buf.at[0, pl.ds(pl.multiple_of(to * piece, 16), piece)], z_buf.at[step - 1], sems, slot, row, to * 2 + core)
        )
        if extra is not None:
            copies.append(remote(cls_z.at[z], cls_z.at[z], sems, slot + 1, row, to * 2 + core))
        slot += 2
    for copy in copies:
        copy.start()
    yield
    finish(copies)
    summed = row_buf[0, pl.ds(pl.multiple_of(z * piece, 16), piece)]
    for step in range(1, nz):
        summed = summed + z_buf[step - 1]
    own = pl.ds(pl.multiple_of(row * part + z * piece, 16), piece)
    fin[core, own] = (summed * scale).astype(jnp.bfloat16)
    if extra is not None:
        across = cls_z[0]
        for i in range(1, nz):
            across = across + cls_z[i]
        outc_ref[...] = across * scale
    copies = []
    for step in range(1, nz):
        to = lax.rem(z + step, nz)
        copies.append(remote(fin.at[core, own], fin.at[core, own], sems, slot, row, to * 2 + core))
        slot += 1
    for copy in copies:
        copy.start()
    yield
    finish(copies)
    copies = []
    for step in range(1, nr):
        to = lax.rem(row + step, nr)
        copies.append(remote(fin.at[core, kept], fin.at[core, kept], sems, slot, to, col))
        slot += 1
    for copy in copies:
        copy.start()
    yield
    finish(copies)
    copy = remote(fin.at[core], fin.at[core], sems, slot, row, twin)
    copy.start()
    yield
    copy.wait()
    out_ref[:, :128] = fin[0].astype(jnp.float32)
    out_ref[:, 128:] = fin[1].astype(jnp.float32)


def reduce_scratch(nr, nz, total, classes, hidden):
    part = total // nr
    return [
        pltpu.VMEM((3, total, 128), jnp.float32),
        pltpu.VMEM((3, nr - 1, part, 128), jnp.float32),
        pltpu.VMEM((3, nz - 1, part // nz, 128), jnp.float32),
        pltpu.VMEM((3, 2, total, 128), jnp.bfloat16),
        pltpu.SemaphoreType.DMA((3, 2, 3 + 3 * (nr - 1) + 3 * (nz - 1))),
        pltpu.VMEM((classes, hidden), jnp.float32),
        pltpu.VMEM((nr, classes, hidden), jnp.float32),
        pltpu.VMEM((nz, classes, hidden), jnp.float32),
    ]


def present(down, right):
    row = lax.axis_index("row") + down
    col = lax.axis_index("col") + right
    rows = lax.axis_size("row")
    cols = lax.axis_size("col")
    return (row >= 0) & (row < rows) & (col >= 0) & (col < cols)


def greet_sides(barrier):
    row = lax.axis_index("row")
    col = lax.axis_index("col")
    for down, right in SIDES:

        @pl.when(present(down, right))
        def _():
            pl.semaphore_signal(barrier, inc=1, device_id=(row + down, col + right), device_id_type=MESH)


def count_sides():
    count = 0
    for down, right in SIDES:
        count = count + jnp.where(present(down, right), 1, 0)
    return count


def side_copies(cells, packs, rim_rows, rim_packs, sems, base, span):
    row = lax.axis_index("row")
    col = lax.axis_index("col")
    pixels = cells.shape[1]
    copies = []
    for index, (down, right) in enumerate(SIDES):
        if right == 0:
            source = cells.at[:, pl.ds(0 if down < 0 else pixels - span, span)]
            target = rim_rows.at[index]
        else:
            source = packs.at[0 if right < 0 else 1]
            target = rim_packs.at[index - 2]
        copies.append((down, right, remote(source, target, sems, base + index, row + down, col + right)))
    return copies


def start_sides(copies):
    for down, right, copy in copies:

        @pl.when(present(down, right))
        def _():
            copy.start()


def finish_sides(copies):
    for down, right, copy in copies:

        @pl.when(present(down, right))
        def _():
            copy.wait_send()

        @pl.when(present(-down, -right))
        def _():
            copy.wait_recv()


def clear_sides(rim_rows, rim_packs):
    for index, (down, right) in enumerate(SIDES):

        @pl.when(jnp.logical_not(present(-down, -right)))
        def _():
            if right == 0:
                rim_rows[index] = jnp.zeros(rim_rows.shape[1:], rim_rows.dtype)
            else:
                rim_packs[index - 2] = jnp.zeros(rim_packs.shape[1:], rim_packs.dtype)


def row_at(index, width):
    return pl.ds(pl.multiple_of(index * width, 128), width)


def pack_sides(cells, packs, rows, width, reach, unroll=1):
    lane = lax.broadcasted_iota(jnp.int32, (cells.shape[0], 128), 1)
    zero = jnp.zeros((cells.shape[0], 128), jnp.float32)

    def step(y, held):
        left = cells[:, pl.ds(pl.multiple_of(y * width, 128), 128)].astype(jnp.float32)
        right = cells[:, pl.ds(pl.multiple_of(y * width + width - 128, 128), 128)].astype(jnp.float32)
        here = (lane >= reach * y) & (lane < reach * y + reach)
        return (
            jnp.where(here, pltpu.roll(left, reach * y, 1), held[0]),
            jnp.where(here, pltpu.roll(right, lax.rem(reach * y + reach, 128), 1), held[1]),
        )

    held = lax.fori_loop(0, rows, step, (zero, zero), unroll=unroll)
    packs[0] = held[0].astype(packs.dtype)
    packs[1] = held[1].astype(packs.dtype)


def rim_tile(pack_left, pack_right, y, reach):
    lane = lax.broadcasted_iota(jnp.int32, pack_left.shape, 1)
    right = pltpu.roll(pack_right.astype(jnp.float32), lax.rem(128 - reach * y, 128), 1)
    left = pltpu.roll(pack_left.astype(jnp.float32), lax.rem(256 - reach - reach * y, 128), 1)
    return jnp.where(lane < reach, right, jnp.where(lane >= 128 - reach, left, 0.0))


def spread(cells, rim_rows, rim_packs, rows, width, reach, emit, unroll=1):
    def top(r, carry):
        tile = rim_tile(rim_packs[5], rim_packs[4], rows - reach + r, reach)
        wide = jnp.concatenate([rim_rows[1, :, row_at(r, width)].astype(jnp.float32), tile], axis=1)
        emit(r, wide)
        return carry

    def centre(r, carry):
        tile = rim_tile(rim_packs[1], rim_packs[0], r, reach)
        wide = jnp.concatenate([cells[:, row_at(r, width)].astype(jnp.float32), tile], axis=1)
        emit(r + reach, wide)
        return carry

    def bottom(r, carry):
        tile = rim_tile(rim_packs[3], rim_packs[2], r, reach)
        wide = jnp.concatenate([rim_rows[0, :, row_at(r, width)].astype(jnp.float32), tile], axis=1)
        emit(r + rows + reach, wide)
        return carry

    lax.fori_loop(0, reach, top, 0, unroll=min(unroll, reach))
    lax.fori_loop(0, rows, centre, 0, unroll=unroll)
    lax.fori_loop(0, reach, bottom, 0, unroll=min(unroll, reach))


def step_kernel(
    nr, nz, rows, width, scale,
    feats, probs, cells, ahead, back, class_in, class_out,
    refined, slope_grad, conv_out, class_grad,
    moved, weights, sweeps, moved_now, feat_packs, feat_rows, feat_rims, packs, prob_rows, prob_rims,
    stacked, steep, hidden_all, chance, error, error_turned, parts, class_part,
    cell_packs, cell_rows, cell_rims, error_packs, error_rows, error_rims, sems,
    core_buf, row_buf, z_buf, fin, reduce_sems, cls_core, cls_row, cls_z,
):
    row = lax.axis_index("row")
    col = lax.axis_index("col")
    core = lax.rem(col, 2)
    z = col // 2
    teacher_channels = feats.shape[0]
    channels, pixels = cells.shape
    hidden_size = class_out.shape[0]
    span = REACH * width
    full_rows = rows * lax.axis_size("row")
    full_cols = width * lax.axis_size("col")
    first_row = row * rows
    first_col = col * width

    barrier = pltpu.get_barrier_semaphore()
    clear_sides(feat_rows, feat_rims)
    clear_sides(cell_rows, cell_rims)
    clear_sides(error_rows, error_rims)
    for sweep in range(ITERS):
        clear_sides(prob_rows.at[sweep], prob_rims.at[sweep])
    greet_sides(barrier)
    pl.semaphore_signal(barrier, inc=1, device_id=(row, z * 2 + 1 - core), device_id_type=MESH)
    for step in range(1, nr):
        pl.semaphore_signal(barrier, inc=1, device_id=(lax.rem(row + step, nr), col), device_id_type=MESH)
    for step in range(1, nz):
        pl.semaphore_signal(barrier, inc=1, device_id=(row, lax.rem(z + step, nz) * 2 + core), device_id_type=MESH)
    pack_sides(feats, feat_packs, rows, width, REACH, 4)
    pack_sides(probs, packs.at[0], rows, width, REACH, rows)
    pl.semaphore_wait(barrier, count_sides() + (nr + nz - 1))
    feat_copies = side_copies(feats, feat_packs, feat_rows, feat_rims, sems, 0, span)
    start_sides(feat_copies)
    copies = side_copies(probs, packs.at[0], prob_rows.at[0], prob_rims.at[0], sems, 8, span)
    start_sides(copies)
    pack_sides(cells, cell_packs, rows, width, 1)
    base = 8 + 8 * ITERS
    cell_copies = side_copies(cells, cell_packs, cell_rows, cell_rims, sems, base, width)
    start_sides(cell_copies)
    finish_sides(feat_copies)

    def emit_feats(r, wide):
        for index, shift in enumerate(SHIFTS):
            turned = wide if shift == 0 else pltpu.roll(wide, (-shift) % wide.shape[1], 1)
            moved[index, :, row_at(r, width)] = turned[:, :width]

    spread(feats, feat_rows, feat_rims, rows, width, REACH, emit_feats)
    place = first_col + lax.broadcasted_iota(jnp.int32, (8, width), 1)

    def weigh(y, carry):
        centre = moved[0, :, row_at(y + REACH, width)]
        total = jnp.ones((8, width), jnp.float32)
        terms = []
        for off_y, off_x in tap_list():
            other = moved[SHIFTS.index(off_x), :, row_at(y + REACH + off_y, width)]
            apart = (centre - other) * (centre - other)
            apart = jnp.sum(apart.reshape(teacher_channels // 8, 8, width), axis=0)
            apart = jnp.broadcast_to(jnp.sum(apart, axis=0, keepdims=True), (8, width))
            at_row = first_row + y + off_y
            inside = (place + off_x >= 0) & (place + off_x < full_cols) & (at_row >= 0) & (at_row < full_rows)
            term = jnp.where(inside, jnp.exp(apart * (-1.0 / teacher_channels)), 0.0)
            terms.append(term)
            total = total + term
        share = 1.0 / total
        weights[0, :, row_at(y, width)] = share
        for index, term in enumerate(terms):
            weights[index + 1, :, row_at(y, width)] = term * share
        return carry

    lax.fori_loop(0, rows, weigh, 0)

    def emit_probs(r, wide):
        for index, shift in enumerate(SHIFTS):
            turned = wide if shift == 0 else pltpu.roll(wide, (-shift) % wide.shape[1], 1)
            moved_now[index, :, row_at(r, width)] = turned[:, :width]

    def stack_into(depth):
        def emit(r, wide):
            for index, shift in enumerate((-1, 0, 1)):
                turned = wide if shift == 0 else pltpu.roll(wide, (-shift) % wide.shape[1], 1)
                stacked[index * depth : (index + 1) * depth, row_at(r, width)] = turned[:, :width].astype(stacked.dtype)

        return emit

    def forward(y, carry):
        here = row_at(y, width)
        pre = jnp.dot(ahead[0], stacked[: 3 * channels, here], preferred_element_type=jnp.float32)
        for tap_row in (1, 2):
            pre = pre + jnp.dot(
                ahead[tap_row], stacked[: 3 * channels, row_at(y + tap_row, width)], preferred_element_type=jnp.float32
            )
        gate = jax.nn.sigmoid(pre)
        hidden = (pre * gate).astype(jnp.bfloat16)
        hidden_all[:, here] = hidden
        steep[:, here] = gate * (1.0 + pre * (1.0 - gate))
        logit = jnp.dot(class_in[...], hidden, preferred_element_type=jnp.float32)
        chance[:, here] = jax.nn.sigmoid(logit)
        return carry

    for sweep in range(ITERS):
        now = probs if sweep == 0 else sweeps.at[sweep - 1]
        later = refined if sweep == ITERS - 1 else sweeps.at[sweep]
        finish_sides(copies)
        spread(now, prob_rows.at[sweep], prob_rims.at[sweep], rows, width, REACH, emit_probs, rows)

        def gather(y, carry):
            running = weights[0, :, row_at(y, width)] * moved_now[0, :, row_at(y + REACH, width)]
            for index, (off_y, off_x) in enumerate(tap_list()):
                running = running + (
                    weights[index + 1, :, row_at(y, width)]
                    * moved_now[SHIFTS.index(off_x), :, row_at(y + REACH + off_y, width)]
                )
            later[:, row_at(y, width)] = running
            return carry

        lax.fori_loop(0, rows, gather, 0, unroll=2)
        if sweep < ITERS - 1:
            pack_sides(later, packs.at[sweep + 1], rows, width, REACH, rows)
            copies = side_copies(
                later, packs.at[sweep + 1], prob_rows.at[sweep + 1], prob_rims.at[sweep + 1], sems, 16 + 8 * sweep, span
            )
            start_sides(copies)
            if sweep == 0:
                finish_sides(cell_copies)
                spread(cells, cell_rows, cell_rims, rows, width, 1, stack_into(channels))
            elif sweep < ITERS - 2:
                lax.fori_loop(0, rows // 2, forward, 0)
            else:
                lax.fori_loop(rows // 2, rows, forward, 0)

    class_part[...] = jnp.zeros_like(class_part)

    def backward(y, carry):
        here = row_at(y, width)
        wrong = (chance[:, here] - refined[:, here]).astype(jnp.bfloat16)
        slope = jnp.dot(class_out[...], wrong, preferred_element_type=jnp.float32) * steep[:, here]
        error[:, here] = slope.astype(jnp.bfloat16)
        error_turned[here, :] = slope.T.astype(jnp.bfloat16)
        class_part[...] += lax.dot_general(
            wrong, hidden_all[:, here], (((1,), (1,)), ((), ())), preferred_element_type=jnp.float32
        )
        return carry

    lax.fori_loop(0, rows, backward, 0, unroll=2)

    def run_chunk(chunk):
        for index in range(3):
            parts[chunk, index * channels : (index + 1) * channels, :] = jnp.dot(
                stacked[index * channels : (index + 1) * channels, chunk * width : chunk * width + pixels],
                error_turned[...],
                preferred_element_type=jnp.float32,
            )
        if parts.shape[1] > 3 * channels:
            parts[chunk, 3 * channels :, :] = jnp.zeros((parts.shape[1] - 3 * channels, parts.shape[2]), jnp.float32)

    def features(y, carry):
        total = jnp.dot(back[0], stacked[: 3 * hidden_size, row_at(y, width)], preferred_element_type=jnp.float32)
        for tap_row in (1, 2):
            total = total + jnp.dot(
                back[tap_row], stacked[: 3 * hidden_size, row_at(y + tap_row, width)], preferred_element_type=jnp.float32
            )
        slope_grad[:, row_at(y, width)] = total.astype(jnp.bfloat16)
        return carry

    def chunk_phases(chunk):
        extra = (class_part, class_grad, cls_core, cls_row, cls_z) if chunk == 0 else None
        return reduce_body(
            nr, nz, scale, parts.at[chunk], conv_out.at[chunk], core_buf.at[chunk], row_buf.at[chunk],
            z_buf.at[chunk], fin.at[chunk], reduce_sems.at[chunk], extra,
        )

    phases = [chunk_phases(chunk) for chunk in range(3)]
    run_chunk(0)
    next(phases[0])
    pack_sides(error, error_packs, rows, width, 1)
    copies = side_copies(error, error_packs, error_rows, error_rims, sems, base + 8, width)
    start_sides(copies)
    run_chunk(1)
    next(phases[0])
    next(phases[1])
    run_chunk(2)
    next(phases[1])
    next(phases[2])
    finish_sides(copies)
    spread(error, error_rows, error_rims, rows, width, 1, stack_into(hidden_size))
    turn = 0
    while phases:
        phases = [phase for phase in phases if next(phase, True) is None]
        if turn < 4:
            lax.fori_loop(turn * rows // 4, (turn + 1) * rows // 4, features, 0)
        turn += 1


def whole_step(feats, probs, cells, conv_weight, class_weight, rows, width):
    teacher_channels = feats.shape[0]
    channels, pixels = cells.shape
    hidden, classes = class_weight.shape
    nr = lax.axis_size("row")
    nz = lax.axis_size("col") // 2
    unit = nr * nz * 16
    span = REACH * width
    wide = (rows + 2) * width
    wider = (rows + 2 * REACH) * width
    total = -(-3 * channels // unit) * unit
    taps = conv_weight.reshape(3, 3, channels, hidden)
    ahead = taps.transpose(0, 3, 1, 2).reshape(3, hidden, 3 * channels)
    back = taps[::-1, ::-1].transpose(0, 2, 1, 3).reshape(3, channels, 3 * hidden)
    f32, bf16 = jnp.float32, jnp.bfloat16
    out = pl.pallas_call(
        functools.partial(step_kernel, nr, nz, rows, width, 1.0 / pixels),
        out_shape=(
            jax.ShapeDtypeStruct((classes, pixels), f32),
            jax.ShapeDtypeStruct((channels, pixels), bf16),
            jax.ShapeDtypeStruct((3, total, hidden), f32),
            jax.ShapeDtypeStruct((classes, hidden), f32),
        ),
        in_specs=[pl.BlockSpec(memory_space=pltpu.VMEM)] * 7,
        out_specs=[pl.BlockSpec(memory_space=pltpu.VMEM)] * 4,
        scratch_shapes=[
            pltpu.VMEM((len(SHIFTS), teacher_channels, wider), f32),
            pltpu.VMEM((25, 8, pixels), f32),
            pltpu.VMEM((ITERS - 1, classes, pixels), f32),
            pltpu.VMEM((len(SHIFTS), classes, wider), f32),
            pltpu.VMEM((2, teacher_channels, 128), bf16),
            pltpu.VMEM((2, teacher_channels, span), bf16),
            pltpu.VMEM((6, teacher_channels, 128), bf16),
            pltpu.VMEM((ITERS, 2, classes, 128), f32),
            pltpu.VMEM((ITERS, 2, classes, span), f32),
            pltpu.VMEM((ITERS, 6, classes, 128), f32),
            pltpu.VMEM((3 * max(channels, hidden), wide), bf16),
            pltpu.VMEM((hidden, pixels), f32),
            pltpu.VMEM((hidden, pixels), bf16),
            pltpu.VMEM((classes, pixels), f32),
            pltpu.VMEM((hidden, pixels), bf16),
            pltpu.VMEM((pixels, hidden), bf16),
            pltpu.VMEM((3, total, hidden), f32),
            pltpu.VMEM((classes, hidden), f32),
            pltpu.VMEM((2, channels, 128), bf16),
            pltpu.VMEM((2, channels, width), bf16),
            pltpu.VMEM((6, channels, 128), bf16),
            pltpu.VMEM((2, hidden, 128), bf16),
            pltpu.VMEM((2, hidden, width), bf16),
            pltpu.VMEM((6, hidden, 128), bf16),
            pltpu.SemaphoreType.DMA((2, 24 + 8 * ITERS)),
        ]
        + reduce_scratch(nr, nz, total, classes, hidden),
        compiler_params=pltpu.CompilerParams(collective_id=0, has_side_effects=True, vmem_limit_bytes=60 * 2**20),
    )(feats, probs, cells, ahead, back, class_weight.T, class_weight)
    return out[0], out[1], out[2][:, : 3 * channels], out[3]


def shards(teacher_feats, teacher_probs, student_feats, conv_weight, class_weight):
    classes, rows, width = teacher_probs.shape
    channels = student_feats.shape[0]
    pixels = rows * width
    refined, feature_grad, grad_conv, grad_class = whole_step(
        teacher_feats.reshape(teacher_feats.shape[0], pixels),
        teacher_probs.reshape(classes, pixels),
        student_feats.reshape(channels, pixels),
        conv_weight,
        class_weight,
        rows,
        width,
    )
    return (
        refined.reshape(classes, rows, width),
        feature_grad.reshape(channels, rows, width),
        grad_conv.reshape(conv_weight.shape),
        grad_class.T,
    )


def solution(mesh):
    in_specs = (P(None, "row", "col"), P(None, "row", "col"), P(None, "row", "col"), P(), P())
    out_specs = (P(None, "row", "col"), P(None, "row", "col"), P(), P())
    return jax.shard_map(shards, mesh=mesh, in_specs=in_specs, out_specs=out_specs, check_vma=False)
```

```python
import functools

import jax
import jax.numpy as jnp
from jax import lax
from jax.experimental import pallas as pl
from jax.experimental.pallas import tpu as pltpu
from jax.sharding import PartitionSpec as P

ITERS = 4
REACH = 4
SHIFTS = (0, 1, 2, 4, -1, -2, -4)
SIDES = ((-1, 0), (1, 0), (0, -1), (0, 1), (-1, -1), (-1, 1), (1, -1), (1, 1))


def tap_list():
    offsets = []
    for radius in (1, 2, 4):
        for step_y in (-1, 0, 1):
            for step_x in (-1, 0, 1):
                if step_y != 0 or step_x != 0:
                    offsets.append((step_y * radius, step_x * radius))
    return offsets


MESH = pl.DeviceIdType.MESH


def remote(src, dst, sems, slot, row, col):
    return pltpu.make_async_remote_copy(
        src_ref=src,
        dst_ref=dst,
        send_sem=sems.at[0, slot],
        recv_sem=sems.at[1, slot],
        device_id=(row, col),
        device_id_type=MESH,
    )


def finish(copies):
    for copy in copies:
        copy.wait()


def reduce_body(nr, nz, scale, g_ref, out_ref, core_buf, row_buf, z_buf, fin, sems, extra=None):
    if extra is not None:
        cls_ref, outc_ref, cls_core, cls_row, cls_z = extra
    row = lax.axis_index("row")
    col = lax.axis_index("col")
    core = lax.rem(col, 2)
    z = col // 2
    twin = z * 2 + 1 - core
    total = g_ref.shape[0]
    part = total // nr
    piece = part // nz
    mine = pl.ds(pl.multiple_of(core * 128, 128), 128)
    other = pl.ds(pl.multiple_of((1 - core) * 128, 128), 128)
    slot = 0
    copies = [remote(g_ref.at[:, other], core_buf, sems, 0, row, twin)]
    if extra is not None:
        copies.append(remote(cls_ref, cls_core, sems, 1, row, twin))
    for copy in copies:
        copy.start()
    yield
    finish(copies)
    slot = 2
    core_buf[...] = core_buf[...] + g_ref[:, mine]
    if extra is not None:
        cls_row[row] = cls_ref[...] + cls_core[...]
    copies = []
    for step in range(1, nr):
        to = lax.rem(row + step, nr)
        copies.append(
            remote(core_buf.at[pl.ds(pl.multiple_of(to * part, 16), part)], row_buf.at[step - 1], sems, slot, to, col)
        )
        if extra is not None:
            copies.append(remote(cls_row.at[row], cls_row.at[row], sems, slot + 1, to, col))
        slot += 2
    for copy in copies:
        copy.start()
    yield
    finish(copies)
    kept = pl.ds(pl.multiple_of(row * part, 16), part)
    summed = core_buf[kept]
    for step in range(1, nr):
        summed = summed + row_buf[step - 1]
    row_buf[0] = summed
    if extra is not None:
        across = cls_row[0]
        for i in range(1, nr):
            across = across + cls_row[i]
        cls_z[z] = across
    copies = []
    for step in range(1, nz):
        to = lax.rem(z + step, nz)
        copies.append(
            remote(row_buf.at[0, pl.ds(pl.multiple_of(to * piece, 16), piece)], z_buf.at[step - 1], sems, slot, row, to * 2 + core)
        )
        if extra is not None:
            copies.append(remote(cls_z.at[z], cls_z.at[z], sems, slot + 1, row, to * 2 + core))
        slot += 2
    for copy in copies:
        copy.start()
    yield
    finish(copies)
    summed = row_buf[0, pl.ds(pl.multiple_of(z * piece, 16), piece)]
    for step in range(1, nz):
        summed = summed + z_buf[step - 1]
    own = pl.ds(pl.multiple_of(row * part + z * piece, 16), piece)
    fin[core, own] = (summed * scale).astype(jnp.bfloat16)
    if extra is not None:
        across = cls_z[0]
        for i in range(1, nz):
            across = across + cls_z[i]
        outc_ref[...] = across * scale
    copies = []
    for step in range(1, nz):
        to = lax.rem(z + step, nz)
        copies.append(remote(fin.at[core, own], fin.at[core, own], sems, slot, row, to * 2 + core))
        slot += 1
    for copy in copies:
        copy.start()
    yield
    finish(copies)
    copies = []
    for step in range(1, nr):
        to = lax.rem(row + step, nr)
        copies.append(remote(fin.at[core, kept], fin.at[core, kept], sems, slot, to, col))
        slot += 1
    for copy in copies:
        copy.start()
    yield
    finish(copies)
    copy = remote(fin.at[core], fin.at[core], sems, slot, row, twin)
    copy.start()
    yield
    copy.wait()
    out_ref[:, :128] = fin[0].astype(jnp.float32)
    out_ref[:, 128:] = fin[1].astype(jnp.float32)


def reduce_scratch(nr, nz, total, classes, hidden):
    part = total // nr
    return [
        pltpu.VMEM((3, total, 128), jnp.float32),
        pltpu.VMEM((3, nr - 1, part, 128), jnp.float32),
        pltpu.VMEM((3, nz - 1, part // nz, 128), jnp.float32),
        pltpu.VMEM((3, 2, total, 128), jnp.bfloat16),
        pltpu.SemaphoreType.DMA((3, 2, 3 + 3 * (nr - 1) + 3 * (nz - 1))),
        pltpu.VMEM((classes, hidden), jnp.float32),
        pltpu.VMEM((nr, classes, hidden), jnp.float32),
        pltpu.VMEM((nz, classes, hidden), jnp.float32),
    ]


def present(down, right):
    row = lax.axis_index("row") + down
    col = lax.axis_index("col") + right
    rows = lax.axis_size("row")
    cols = lax.axis_size("col")
    return (row >= 0) & (row < rows) & (col >= 0) & (col < cols)


def greet_sides(barrier):
    row = lax.axis_index("row")
    col = lax.axis_index("col")
    for down, right in SIDES:

        @pl.when(present(down, right))
        def _():
            pl.semaphore_signal(barrier, inc=1, device_id=(row + down, col + right), device_id_type=MESH)


def count_sides():
    count = 0
    for down, right in SIDES:
        count = count + jnp.where(present(down, right), 1, 0)
    return count


def side_copies(cells, packs, rim_rows, rim_packs, sems, base, span):
    row = lax.axis_index("row")
    col = lax.axis_index("col")
    pixels = cells.shape[1]
    copies = []
    for index, (down, right) in enumerate(SIDES):
        if right == 0:
            source = cells.at[:, pl.ds(0 if down < 0 else pixels - span, span)]
            target = rim_rows.at[index]
        else:
            source = packs.at[0 if right < 0 else 1]
            target = rim_packs.at[index - 2]
        copies.append((down, right, remote(source, target, sems, base + index, row + down, col + right)))
    return copies


def start_sides(copies):
    for down, right, copy in copies:

        @pl.when(present(down, right))
        def _():
            copy.start()


def finish_sides(copies):
    for down, right, copy in copies:

        @pl.when(present(down, right))
        def _():
            copy.wait_send()

        @pl.when(present(-down, -right))
        def _():
            copy.wait_recv()


def clear_sides(rim_rows, rim_packs):
    for index, (down, right) in enumerate(SIDES):

        @pl.when(jnp.logical_not(present(-down, -right)))
        def _():
            if right == 0:
                rim_rows[index] = jnp.zeros(rim_rows.shape[1:], rim_rows.dtype)
            else:
                rim_packs[index - 2] = jnp.zeros(rim_packs.shape[1:], rim_packs.dtype)


def row_at(index, width):
    return pl.ds(pl.multiple_of(index * width, 128), width)


def pack_sides(cells, packs, rows, width, reach, unroll=1):
    lane = lax.broadcasted_iota(jnp.int32, (cells.shape[0], 128), 1)
    zero = jnp.zeros((cells.shape[0], 128), jnp.float32)

    def step(y, held):
        left = cells[:, pl.ds(pl.multiple_of(y * width, 128), 128)].astype(jnp.float32)
        right = cells[:, pl.ds(pl.multiple_of(y * width + width - 128, 128), 128)].astype(jnp.float32)
        here = (lane >= reach * y) & (lane < reach * y + reach)
        return (
            jnp.where(here, pltpu.roll(left, reach * y, 1), held[0]),
            jnp.where(here, pltpu.roll(right, lax.rem(reach * y + reach, 128), 1), held[1]),
        )

    held = lax.fori_loop(0, rows, step, (zero, zero), unroll=unroll)
    packs[0] = held[0].astype(packs.dtype)
    packs[1] = held[1].astype(packs.dtype)


def turn_packs(packs, turned):
    for side in range(2):
        turned[side] = packs[side].T[: turned.shape[1]].astype(turned.dtype)


def unturn_rims(turned, rim_packs):
    for index in range(6):
        rows = turned[index].astype(jnp.float32)
        rest = jnp.zeros((128 - rows.shape[0], rows.shape[1]), jnp.float32)
        rim_packs[index] = jnp.concatenate([rows, rest], axis=0).T


def rim_tile(pack_left, pack_right, y, reach):
    lane = lax.broadcasted_iota(jnp.int32, pack_left.shape, 1)
    right = pltpu.roll(pack_right.astype(jnp.float32), lax.rem(128 - reach * y, 128), 1)
    left = pltpu.roll(pack_left.astype(jnp.float32), lax.rem(256 - reach - reach * y, 128), 1)
    return jnp.where(lane < reach, right, jnp.where(lane >= 128 - reach, left, 0.0))


def spread(cells, rim_rows, rim_packs, rows, width, reach, emit, unroll=1):
    def top(r, carry):
        tile = rim_tile(rim_packs[5], rim_packs[4], rows - reach + r, reach)
        wide = jnp.concatenate([rim_rows[1, :, row_at(r, width)].astype(jnp.float32), tile], axis=1)
        emit(r, wide)
        return carry

    def centre(r, carry):
        tile = rim_tile(rim_packs[1], rim_packs[0], r, reach)
        wide = jnp.concatenate([cells[:, row_at(r, width)].astype(jnp.float32), tile], axis=1)
        emit(r + reach, wide)
        return carry

    def bottom(r, carry):
        tile = rim_tile(rim_packs[3], rim_packs[2], r, reach)
        wide = jnp.concatenate([rim_rows[0, :, row_at(r, width)].astype(jnp.float32), tile], axis=1)
        emit(r + rows + reach, wide)
        return carry

    lax.fori_loop(0, reach, top, 0, unroll=min(unroll, reach))
    lax.fori_loop(0, rows, centre, 0, unroll=unroll)
    lax.fori_loop(0, reach, bottom, 0, unroll=min(unroll, reach))


def step_kernel(
    nr, nz, rows, width, scale,
    feats, probs, cells, conv_weight, class_in,
    refined, slope_grad, conv_out, class_grad,
    ahead, back, class_out, wide_packs, wide_rims, moved, weights, sweeps, moved_now, feat_packs, feat_rows, feat_rims, packs, prob_rows, prob_rims,
    stacked, steep, hidden_all, chance, error, error_turned, parts, class_part,
    cell_packs, cell_rows, cell_rims, error_packs, error_rows, error_rims, sems,
    core_buf, row_buf, z_buf, fin, reduce_sems, cls_core, cls_row, cls_z,
):
    row = lax.axis_index("row")
    col = lax.axis_index("col")
    core = lax.rem(col, 2)
    z = col // 2
    teacher_channels = feats.shape[0]
    channels, pixels = cells.shape
    hidden_size = class_in.shape[1]
    span = REACH * width
    full_rows = rows * lax.axis_size("row")
    full_cols = width * lax.axis_size("col")
    first_row = row * rows
    first_col = col * width

    barrier = pltpu.get_barrier_semaphore()
    clear_sides(feat_rows, feat_rims)
    clear_sides(cell_rows, cell_rims)
    clear_sides(error_rows, error_rims)
    for sweep in range(ITERS):
        clear_sides(prob_rows.at[sweep], prob_rims.at[sweep])
    greet_sides(barrier)
    pl.semaphore_signal(barrier, inc=1, device_id=(row, z * 2 + 1 - core), device_id_type=MESH)
    for step in range(1, nr):
        pl.semaphore_signal(barrier, inc=1, device_id=(lax.rem(row + step, nr), col), device_id_type=MESH)
    for step in range(1, nz):
        pl.semaphore_signal(barrier, inc=1, device_id=(row, lax.rem(z + step, nz) * 2 + core), device_id_type=MESH)
    pack_sides(feats, feat_packs, rows, width, REACH, 4)
    pack_sides(probs, packs.at[0], rows, width, REACH, rows)
    pl.semaphore_wait(barrier, count_sides() + (nr + nz - 1))
    feat_copies = side_copies(feats, feat_packs, feat_rows, feat_rims, sems, 0, span)
    start_sides(feat_copies)
    copies = side_copies(probs, packs.at[0], prob_rows.at[0], prob_rims.at[0], sems, 8, span)
    start_sides(copies)
    pack_sides(cells, wide_packs, rows, width, 1)
    turn_packs(wide_packs, cell_packs)
    base = 8 + 8 * ITERS
    cell_copies = side_copies(cells, cell_packs, cell_rows, cell_rims, sems, base, width)
    start_sides(cell_copies)
    for tap in range(9):
        index = tap % 3
        ahead[tap // 3, :, index * channels : (index + 1) * channels] = (
            conv_weight[tap].astype(jnp.float32).T.astype(jnp.bfloat16)
        )
        back[tap // 3, :, index * hidden_size : (index + 1) * hidden_size] = conv_weight[8 - tap]
    class_out[...] = class_in[...].astype(jnp.float32).T.astype(jnp.bfloat16)
    finish_sides(feat_copies)

    def emit_feats(r, wide):
        for index, shift in enumerate(SHIFTS):
            turned = wide if shift == 0 else pltpu.roll(wide, (-shift) % wide.shape[1], 1)
            moved[index, :, row_at(r, width)] = turned[:, :width]

    spread(feats, feat_rows, feat_rims, rows, width, REACH, emit_feats)
    place = first_col + lax.broadcasted_iota(jnp.int32, (8, width), 1)

    def weigh(y, carry):
        centre = moved[0, :, row_at(y + REACH, width)]
        total = jnp.ones((8, width), jnp.float32)
        terms = []
        for off_y, off_x in tap_list():
            other = moved[SHIFTS.index(off_x), :, row_at(y + REACH + off_y, width)]
            apart = (centre - other) * (centre - other)
            apart = jnp.sum(apart.reshape(teacher_channels // 8, 8, width), axis=0)
            apart = jnp.broadcast_to(jnp.sum(apart, axis=0, keepdims=True), (8, width))
            at_row = first_row + y + off_y
            inside = (place + off_x >= 0) & (place + off_x < full_cols) & (at_row >= 0) & (at_row < full_rows)
            term = jnp.where(inside, jnp.exp(apart * (-1.0 / teacher_channels)), 0.0)
            terms.append(term)
            total = total + term
        share = 1.0 / total
        weights[0, :, row_at(y, width)] = share
        for index, term in enumerate(terms):
            weights[index + 1, :, row_at(y, width)] = term * share
        return carry

    lax.fori_loop(0, rows, weigh, 0)

    def emit_probs(r, wide):
        for index, shift in enumerate(SHIFTS):
            turned = wide if shift == 0 else pltpu.roll(wide, (-shift) % wide.shape[1], 1)
            moved_now[index, :, row_at(r, width)] = turned[:, :width]

    def stack_into(depth):
        def emit(r, wide):
            for index, shift in enumerate((-1, 0, 1)):
                turned = wide if shift == 0 else pltpu.roll(wide, (-shift) % wide.shape[1], 1)
                stacked[index * depth : (index + 1) * depth, row_at(r, width)] = turned[:, :width].astype(stacked.dtype)

        return emit

    def forward(y, carry):
        here = row_at(y, width)
        pre = jnp.dot(ahead[0], stacked[: 3 * channels, here], preferred_element_type=jnp.float32)
        for tap_row in (1, 2):
            pre = pre + jnp.dot(
                ahead[tap_row], stacked[: 3 * channels, row_at(y + tap_row, width)], preferred_element_type=jnp.float32
            )
        gate = jax.nn.sigmoid(pre)
        hidden = (pre * gate).astype(jnp.bfloat16)
        hidden_all[:, here] = hidden
        steep[:, here] = gate * (1.0 + pre * (1.0 - gate))
        logit = jnp.dot(class_in[...], hidden, preferred_element_type=jnp.float32)
        chance[:, here] = jax.nn.sigmoid(logit)
        return carry

    for sweep in range(ITERS):
        now = probs if sweep == 0 else sweeps.at[sweep - 1]
        later = refined if sweep == ITERS - 1 else sweeps.at[sweep]
        finish_sides(copies)
        spread(now, prob_rows.at[sweep], prob_rims.at[sweep], rows, width, REACH, emit_probs, rows)

        def gather(y, carry):
            running = weights[0, :, row_at(y, width)] * moved_now[0, :, row_at(y + REACH, width)]
            for index, (off_y, off_x) in enumerate(tap_list()):
                running = running + (
                    weights[index + 1, :, row_at(y, width)]
                    * moved_now[SHIFTS.index(off_x), :, row_at(y + REACH + off_y, width)]
                )
            later[:, row_at(y, width)] = running
            return carry

        lax.fori_loop(0, rows, gather, 0, unroll=2)
        if sweep < ITERS - 1:
            pack_sides(later, packs.at[sweep + 1], rows, width, REACH, rows)
            copies = side_copies(
                later, packs.at[sweep + 1], prob_rows.at[sweep + 1], prob_rims.at[sweep + 1], sems, 16 + 8 * sweep, span
            )
            start_sides(copies)
            if sweep == 0:
                finish_sides(cell_copies)
                unturn_rims(cell_rims, wide_rims)
                spread(cells, cell_rows, wide_rims, rows, width, 1, stack_into(channels))
            elif sweep < ITERS - 2:
                lax.fori_loop(0, rows // 2, forward, 0)
            else:
                lax.fori_loop(rows // 2, rows, forward, 0)

    class_part[...] = jnp.zeros_like(class_part)

    def backward(y, carry):
        here = row_at(y, width)
        wrong = (chance[:, here] - refined[:, here]).astype(jnp.bfloat16)
        slope = jnp.dot(class_out[...], wrong, preferred_element_type=jnp.float32) * steep[:, here]
        error[:, here] = slope.astype(jnp.bfloat16)
        error_turned[here, :] = slope.T.astype(jnp.bfloat16)
        class_part[...] += lax.dot_general(
            wrong, hidden_all[:, here], (((1,), (1,)), ((), ())), preferred_element_type=jnp.float32
        )
        return carry

    lax.fori_loop(0, rows, backward, 0, unroll=2)

    def run_chunk(chunk):
        for index in range(3):
            parts[chunk, index * channels : (index + 1) * channels, :] = jnp.dot(
                stacked[index * channels : (index + 1) * channels, chunk * width : chunk * width + pixels],
                error_turned[...],
                preferred_element_type=jnp.float32,
            )
        if parts.shape[1] > 3 * channels:
            parts[chunk, 3 * channels :, :] = jnp.zeros((parts.shape[1] - 3 * channels, parts.shape[2]), jnp.float32)

    def features(y, carry):
        total = jnp.dot(back[0], stacked[: 3 * hidden_size, row_at(y, width)], preferred_element_type=jnp.float32)
        for tap_row in (1, 2):
            total = total + jnp.dot(
                back[tap_row], stacked[: 3 * hidden_size, row_at(y + tap_row, width)], preferred_element_type=jnp.float32
            )
        slope_grad[:, row_at(y, width)] = total.astype(jnp.bfloat16)
        return carry

    def chunk_phases(chunk):
        extra = (class_part, class_grad, cls_core, cls_row, cls_z) if chunk == 0 else None
        return reduce_body(
            nr, nz, scale, parts.at[chunk], conv_out.at[chunk], core_buf.at[chunk], row_buf.at[chunk],
            z_buf.at[chunk], fin.at[chunk], reduce_sems.at[chunk], extra,
        )

    phases = [chunk_phases(chunk) for chunk in range(3)]
    pack_sides(error, wide_packs, rows, width, 1)
    turn_packs(wide_packs, error_packs)
    copies = side_copies(error, error_packs, error_rows, error_rims, sems, base + 8, width)
    start_sides(copies)
    run_chunk(0)
    next(phases[0])
    run_chunk(1)
    next(phases[0])
    next(phases[1])
    run_chunk(2)
    next(phases[1])
    next(phases[2])
    finish_sides(copies)
    unturn_rims(error_rims, wide_rims)
    spread(error, error_rows, wide_rims, rows, width, 1, stack_into(hidden_size))
    turn = 0
    while phases:
        phases = [phase for phase in phases if next(phase, True) is None]
        if turn < 4:
            lax.fori_loop(turn * rows // 4, (turn + 1) * rows // 4, features, 0)
        turn += 1


def whole_step(feats, probs, cells, conv_weight, class_weight, rows, width):
    teacher_channels = feats.shape[0]
    channels, pixels = cells.shape
    hidden, classes = class_weight.shape
    nr = lax.axis_size("row")
    nz = lax.axis_size("col") // 2
    unit = nr * nz * 16
    span = REACH * width
    wide = (rows + 2) * width
    wider = (rows + 2 * REACH) * width
    total = -(-3 * channels // unit) * unit
    turned = -(-rows // 16) * 16
    f32, bf16 = jnp.float32, jnp.bfloat16
    out = pl.pallas_call(
        functools.partial(step_kernel, nr, nz, rows, width, 1.0 / pixels),
        out_shape=(
            jax.ShapeDtypeStruct((classes, pixels), f32),
            jax.ShapeDtypeStruct((channels, pixels), bf16),
            jax.ShapeDtypeStruct((3, total, hidden), f32),
            jax.ShapeDtypeStruct((classes, hidden), f32),
        ),
        in_specs=[pl.BlockSpec(memory_space=pltpu.VMEM)] * 5,
        out_specs=[pl.BlockSpec(memory_space=pltpu.VMEM)] * 4,
        scratch_shapes=[
            pltpu.VMEM((3, hidden, 3 * channels), bf16),
            pltpu.VMEM((3, channels, 3 * hidden), bf16),
            pltpu.VMEM((hidden, classes), bf16),
            pltpu.VMEM((2, max(channels, hidden), 128), f32),
            pltpu.VMEM((6, max(channels, hidden), 128), f32),
            pltpu.VMEM((len(SHIFTS), teacher_channels, wider), f32),
            pltpu.VMEM((25, 8, pixels), f32),
            pltpu.VMEM((ITERS - 1, classes, pixels), f32),
            pltpu.VMEM((len(SHIFTS), classes, wider), f32),
            pltpu.VMEM((2, teacher_channels, 128), bf16),
            pltpu.VMEM((2, teacher_channels, span), bf16),
            pltpu.VMEM((6, teacher_channels, 128), bf16),
            pltpu.VMEM((ITERS, 2, classes, 128), f32),
            pltpu.VMEM((ITERS, 2, classes, span), f32),
            pltpu.VMEM((ITERS, 6, classes, 128), f32),
            pltpu.VMEM((3 * max(channels, hidden), wide), bf16),
            pltpu.VMEM((hidden, pixels), f32),
            pltpu.VMEM((hidden, pixels), bf16),
            pltpu.VMEM((classes, pixels), f32),
            pltpu.VMEM((hidden, pixels), bf16),
            pltpu.VMEM((pixels, hidden), bf16),
            pltpu.VMEM((3, total, hidden), f32),
            pltpu.VMEM((classes, hidden), f32),
            pltpu.VMEM((2, turned, channels), bf16),
            pltpu.VMEM((2, channels, width), bf16),
            pltpu.VMEM((6, turned, channels), bf16),
            pltpu.VMEM((2, turned, hidden), bf16),
            pltpu.VMEM((2, hidden, width), bf16),
            pltpu.VMEM((6, turned, hidden), bf16),
            pltpu.SemaphoreType.DMA((2, 24 + 8 * ITERS)),
        ]
        + reduce_scratch(nr, nz, total, classes, hidden),
        compiler_params=pltpu.CompilerParams(collective_id=0, has_side_effects=True, vmem_limit_bytes=60 * 2**20),
    )(feats, probs, cells, conv_weight, class_weight.T)
    return out[0], out[1], out[2][:, : 3 * channels], out[3]


def shards(teacher_feats, teacher_probs, student_feats, conv_weight, class_weight):
    classes, rows, width = teacher_probs.shape
    channels = student_feats.shape[0]
    pixels = rows * width
    refined, feature_grad, grad_conv, grad_class = whole_step(
        teacher_feats.reshape(teacher_feats.shape[0], pixels),
        teacher_probs.reshape(classes, pixels),
        student_feats.reshape(channels, pixels),
        conv_weight,
        class_weight,
        rows,
        width,
    )
    return (
        refined.reshape(classes, rows, width),
        feature_grad.reshape(channels, rows, width),
        grad_conv.reshape(conv_weight.shape),
        grad_class.T,
    )


def solution(mesh):
    in_specs = (P(None, "row", "col"), P(None, "row", "col"), P(None, "row", "col"), P(), P())
    out_specs = (P(None, "row", "col"), P(None, "row", "col"), P(), P())
    return jax.shard_map(shards, mesh=mesh, in_specs=in_specs, out_specs=out_specs, check_vma=False)
```

```python
import functools

import jax
import jax.numpy as jnp
from jax import lax
from jax.experimental import pallas as pl
from jax.experimental.pallas import tpu as pltpu
from jax.sharding import PartitionSpec as P

ITERS = 4
REACH = 4
SHIFTS = (0, 1, 2, 4, -1, -2, -4)
SIDES = ((-1, 0), (1, 0), (0, -1), (0, 1), (-1, -1), (-1, 1), (1, -1), (1, 1))


def tap_list():
    offsets = []
    for radius in (1, 2, 4):
        for step_y in (-1, 0, 1):
            for step_x in (-1, 0, 1):
                if step_y != 0 or step_x != 0:
                    offsets.append((step_y * radius, step_x * radius))
    return offsets


MESH = pl.DeviceIdType.MESH


def remote(src, dst, sems, slot, row, col):
    return pltpu.make_async_remote_copy(
        src_ref=src,
        dst_ref=dst,
        send_sem=sems.at[0, slot],
        recv_sem=sems.at[1, slot],
        device_id=(row, col),
        device_id_type=MESH,
    )


def finish(copies):
    for copy in copies:
        copy.wait()


def reduce_body(nr, nz, scale, g_ref, out_ref, core_buf, row_buf, z_buf, fin, sems, extra=None):
    if extra is not None:
        cls_ref, outc_ref, cls_core, cls_row, cls_z = extra
    row = lax.axis_index("row")
    col = lax.axis_index("col")
    core = lax.rem(col, 2)
    z = col // 2
    twin = z * 2 + 1 - core
    total = g_ref.shape[0]
    part = total // nr
    piece = part // nz
    mine = pl.ds(pl.multiple_of(core * 128, 128), 128)
    other = pl.ds(pl.multiple_of((1 - core) * 128, 128), 128)
    slot = 0
    copies = [remote(g_ref.at[:, other], core_buf, sems, 0, row, twin)]
    if extra is not None:
        copies.append(remote(cls_ref, cls_core, sems, 1, row, twin))
    for copy in copies:
        copy.start()
    yield
    finish(copies)
    slot = 2
    core_buf[...] = core_buf[...] + g_ref[:, mine]
    if extra is not None:
        cls_row[row] = cls_ref[...] + cls_core[...]
    copies = []
    for step in range(1, nr):
        to = lax.rem(row + step, nr)
        copies.append(
            remote(core_buf.at[pl.ds(pl.multiple_of(to * part, 16), part)], row_buf.at[step - 1], sems, slot, to, col)
        )
        if extra is not None:
            copies.append(remote(cls_row.at[row], cls_row.at[row], sems, slot + 1, to, col))
        slot += 2
    for copy in copies:
        copy.start()
    yield
    finish(copies)
    kept = pl.ds(pl.multiple_of(row * part, 16), part)
    summed = core_buf[kept]
    for step in range(1, nr):
        summed = summed + row_buf[step - 1]
    row_buf[0] = summed
    if extra is not None:
        across = cls_row[0]
        for i in range(1, nr):
            across = across + cls_row[i]
        cls_z[z] = across
    copies = []
    for step in range(1, nz):
        to = lax.rem(z + step, nz)
        copies.append(
            remote(row_buf.at[0, pl.ds(pl.multiple_of(to * piece, 16), piece)], z_buf.at[step - 1], sems, slot, row, to * 2 + core)
        )
        if extra is not None:
            copies.append(remote(cls_z.at[z], cls_z.at[z], sems, slot + 1, row, to * 2 + core))
        slot += 2
    for copy in copies:
        copy.start()
    yield
    finish(copies)
    summed = row_buf[0, pl.ds(pl.multiple_of(z * piece, 16), piece)]
    for step in range(1, nz):
        summed = summed + z_buf[step - 1]
    own = pl.ds(pl.multiple_of(row * part + z * piece, 16), piece)
    fin[core, own] = (summed * scale).astype(jnp.bfloat16)
    if extra is not None:
        across = cls_z[0]
        for i in range(1, nz):
            across = across + cls_z[i]
        outc_ref[...] = across * scale
    copies = []
    for step in range(1, nz):
        to = lax.rem(z + step, nz)
        copies.append(remote(fin.at[core, own], fin.at[core, own], sems, slot, row, to * 2 + core))
        slot += 1
    for copy in copies:
        copy.start()
    yield
    finish(copies)
    copies = []
    for step in range(1, nr):
        to = lax.rem(row + step, nr)
        copies.append(remote(fin.at[core, kept], fin.at[core, kept], sems, slot, to, col))
        slot += 1
    for copy in copies:
        copy.start()
    yield
    finish(copies)
    copy = remote(fin.at[core], fin.at[core], sems, slot, row, twin)
    copy.start()
    yield
    copy.wait()
    out_ref[:, :128] = fin[0].astype(jnp.float32)
    out_ref[:, 128:] = fin[1].astype(jnp.float32)


def reduce_scratch(nr, nz, total, classes, hidden):
    part = total // nr
    return [
        pltpu.VMEM((3, total, 128), jnp.float32),
        pltpu.VMEM((3, nr - 1, part, 128), jnp.float32),
        pltpu.VMEM((3, nz - 1, part // nz, 128), jnp.float32),
        pltpu.VMEM((3, 2, total, 128), jnp.bfloat16),
        pltpu.SemaphoreType.DMA((3, 2, 3 + 3 * (nr - 1) + 3 * (nz - 1))),
        pltpu.VMEM((classes, hidden), jnp.float32),
        pltpu.VMEM((nr, classes, hidden), jnp.float32),
        pltpu.VMEM((nz, classes, hidden), jnp.float32),
    ]


def present(down, right):
    row = lax.axis_index("row") + down
    col = lax.axis_index("col") + right
    rows = lax.axis_size("row")
    cols = lax.axis_size("col")
    return (row >= 0) & (row < rows) & (col >= 0) & (col < cols)


def greet_sides(barrier):
    row = lax.axis_index("row")
    col = lax.axis_index("col")
    for down, right in SIDES:

        @pl.when(present(down, right))
        def _():
            pl.semaphore_signal(barrier, inc=1, device_id=(row + down, col + right), device_id_type=MESH)


def count_sides():
    count = 0
    for down, right in SIDES:
        count = count + jnp.where(present(down, right), 1, 0)
    return count


def side_copies(cells, packs, rim_rows, rim_packs, sems, base, span):
    row = lax.axis_index("row")
    col = lax.axis_index("col")
    pixels = cells.shape[1]
    copies = []
    for index, (down, right) in enumerate(SIDES):
        if right == 0:
            source = cells.at[:, pl.ds(0 if down < 0 else pixels - span, span)]
            target = rim_rows.at[index]
        else:
            source = packs.at[0 if right < 0 else 1]
            target = rim_packs.at[index - 2]
        copies.append((down, right, remote(source, target, sems, base + index, row + down, col + right)))
    return copies


def start_sides(copies):
    for down, right, copy in copies:

        @pl.when(present(down, right))
        def _():
            copy.start()


def finish_sides(copies):
    for down, right, copy in copies:

        @pl.when(present(down, right))
        def _():
            copy.wait_send()

        @pl.when(present(-down, -right))
        def _():
            copy.wait_recv()


def clear_sides(rim_rows, rim_packs):
    for index, (down, right) in enumerate(SIDES):

        @pl.when(jnp.logical_not(present(-down, -right)))
        def _():
            if right == 0:
                rim_rows[index] = jnp.zeros(rim_rows.shape[1:], rim_rows.dtype)
            else:
                rim_packs[index - 2] = jnp.zeros(rim_packs.shape[1:], rim_packs.dtype)


def row_at(index, width):
    return pl.ds(pl.multiple_of(index * width, 128), width)


def pack_sides(cells, packs, rows, width, reach, unroll=1):
    lane = lax.broadcasted_iota(jnp.int32, (cells.shape[0], 128), 1)
    zero = jnp.zeros((cells.shape[0], 128), jnp.float32)

    def step(y, held):
        left = cells[:, pl.ds(pl.multiple_of(y * width, 128), 128)].astype(jnp.float32)
        right = cells[:, pl.ds(pl.multiple_of(y * width + width - 128, 128), 128)].astype(jnp.float32)
        here = (lane >= reach * y) & (lane < reach * y + reach)
        return (
            jnp.where(here, pltpu.roll(left, reach * y, 1), held[0]),
            jnp.where(here, pltpu.roll(right, lax.rem(reach * y + reach, 128), 1), held[1]),
        )

    held = lax.fori_loop(0, rows, step, (zero, zero), unroll=unroll)
    packs[0] = held[0].astype(packs.dtype)
    packs[1] = held[1].astype(packs.dtype)


def turn_packs(packs, turned):
    for side in range(2):
        turned[side] = packs[side].T[: turned.shape[1]].astype(turned.dtype)


def unturn_rims(turned, rim_packs):
    for index in range(6):
        rows = turned[index].astype(jnp.float32)
        rest = jnp.zeros((128 - rows.shape[0], rows.shape[1]), jnp.float32)
        rim_packs[index] = jnp.concatenate([rows, rest], axis=0).T


def rim_tile(pack_left, pack_right, y, reach):
    lane = lax.broadcasted_iota(jnp.int32, pack_left.shape, 1)
    right = pltpu.roll(pack_right.astype(jnp.float32), lax.rem(128 - reach * y, 128), 1)
    left = pltpu.roll(pack_left.astype(jnp.float32), lax.rem(256 - reach - reach * y, 128), 1)
    return jnp.where(lane < reach, right, jnp.where(lane >= 128 - reach, left, 0.0))


def spread(cells, rim_rows, rim_packs, rows, width, reach, emit, unroll=1):
    def top(r, carry):
        tile = rim_tile(rim_packs[5], rim_packs[4], rows - reach + r, reach)
        wide = jnp.concatenate([rim_rows[1, :, row_at(r, width)].astype(jnp.float32), tile], axis=1)
        emit(r, wide)
        return carry

    def centre(r, carry):
        tile = rim_tile(rim_packs[1], rim_packs[0], r, reach)
        wide = jnp.concatenate([cells[:, row_at(r, width)].astype(jnp.float32), tile], axis=1)
        emit(r + reach, wide)
        return carry

    def bottom(r, carry):
        tile = rim_tile(rim_packs[3], rim_packs[2], r, reach)
        wide = jnp.concatenate([rim_rows[0, :, row_at(r, width)].astype(jnp.float32), tile], axis=1)
        emit(r + rows + reach, wide)
        return carry

    lax.fori_loop(0, reach, top, 0, unroll=min(unroll, reach))
    lax.fori_loop(0, rows, centre, 0, unroll=unroll)
    lax.fori_loop(0, reach, bottom, 0, unroll=min(unroll, reach))


def step_kernel(
    nr, nz, rows, width, scale,
    feats, probs, cells, conv_weight, class_in,
    refined, slope_grad, conv_out, class_grad,
    ahead, back, class_out, wide_packs, wide_rims, moved, weights, sweeps, moved_now, feat_packs, feat_rows, feat_rims, packs, prob_rows, prob_rims,
    stacked, steep, hidden_all, chance, error, error_turned, parts, class_part,
    cell_packs, cell_rows, cell_rims, error_packs, error_rows, error_rims, sems,
    core_buf, row_buf, z_buf, fin, reduce_sems, cls_core, cls_row, cls_z,
):
    row = lax.axis_index("row")
    col = lax.axis_index("col")
    core = lax.rem(col, 2)
    z = col // 2
    teacher_channels = feats.shape[0]
    channels, pixels = cells.shape
    hidden_size = class_in.shape[1]
    span = REACH * width
    full_rows = rows * lax.axis_size("row")
    full_cols = width * lax.axis_size("col")
    first_row = row * rows
    first_col = col * width

    barrier = pltpu.get_barrier_semaphore()
    clear_sides(feat_rows, feat_rims)
    clear_sides(cell_rows, cell_rims)
    clear_sides(error_rows, error_rims)
    for sweep in range(ITERS):
        clear_sides(prob_rows.at[sweep], prob_rims.at[sweep])
    greet_sides(barrier)
    pl.semaphore_signal(barrier, inc=1, device_id=(row, z * 2 + 1 - core), device_id_type=MESH)
    for step in range(1, nr):
        pl.semaphore_signal(barrier, inc=1, device_id=(lax.rem(row + step, nr), col), device_id_type=MESH)
    for step in range(1, nz):
        pl.semaphore_signal(barrier, inc=1, device_id=(row, lax.rem(z + step, nz) * 2 + core), device_id_type=MESH)
    pack_sides(feats, feat_packs, rows, width, REACH, 4)
    pack_sides(probs, packs.at[0], rows, width, REACH, rows)
    pl.semaphore_wait(barrier, count_sides() + (nr + nz - 1))
    feat_copies = side_copies(feats, feat_packs, feat_rows, feat_rims, sems, 0, span)
    start_sides(feat_copies)
    copies = side_copies(probs, packs.at[0], prob_rows.at[0], prob_rims.at[0], sems, 8, span)
    start_sides(copies)
    pack_sides(cells, wide_packs, rows, width, 1)
    turn_packs(wide_packs, cell_packs)
    base = 8 + 8 * ITERS
    cell_copies = side_copies(cells, cell_packs, cell_rows, cell_rims, sems, base, width)
    start_sides(cell_copies)
    for tap in range(9):
        index = tap % 3
        ahead[tap // 3, :, index * channels : (index + 1) * channels] = (
            conv_weight[tap].astype(jnp.float32).T.astype(jnp.bfloat16)
        )
        back[tap // 3, :, index * hidden_size : (index + 1) * hidden_size] = conv_weight[8 - tap]
    class_out[...] = class_in[...].astype(jnp.float32).T.astype(jnp.bfloat16)
    finish_sides(feat_copies)

    def emit_feats(r, wide):
        for index, shift in enumerate(SHIFTS):
            turned = wide if shift == 0 else pltpu.roll(wide, (-shift) % wide.shape[1], 1)
            moved[index, :, row_at(r, width)] = turned[:, :width]

    spread(feats, feat_rows, feat_rims, rows, width, REACH, emit_feats, 2)
    place = first_col + lax.broadcasted_iota(jnp.int32, (8, width), 1)

    def weigh(y, carry):
        centre = moved[0, :, row_at(y + REACH, width)]
        total = jnp.ones((8, width), jnp.float32)
        terms = []
        for off_y, off_x in tap_list():
            other = moved[SHIFTS.index(off_x), :, row_at(y + REACH + off_y, width)]
            apart = (centre - other) * (centre - other)
            apart = jnp.sum(apart.reshape(teacher_channels // 8, 8, width), axis=0)
            apart = jnp.broadcast_to(jnp.sum(apart, axis=0, keepdims=True), (8, width))
            at_row = first_row + y + off_y
            inside = (place + off_x >= 0) & (place + off_x < full_cols) & (at_row >= 0) & (at_row < full_rows)
            term = jnp.where(inside, jnp.exp(apart * (-1.0 / teacher_channels)), 0.0)
            terms.append(term)
            total = total + term
        share = 1.0 / total
        weights[0, :, row_at(y, width)] = share
        for index, term in enumerate(terms):
            weights[index + 1, :, row_at(y, width)] = term * share
        return carry

    lax.fori_loop(0, rows, weigh, 0)

    def emit_probs(r, wide):
        for index, shift in enumerate(SHIFTS):
            turned = wide if shift == 0 else pltpu.roll(wide, (-shift) % wide.shape[1], 1)
            moved_now[index, :, row_at(r, width)] = turned[:, :width]

    def stack_into(depth):
        def emit(r, wide):
            for index, shift in enumerate((-1, 0, 1)):
                turned = wide if shift == 0 else pltpu.roll(wide, (-shift) % wide.shape[1], 1)
                stacked[index * depth : (index + 1) * depth, row_at(r, width)] = turned[:, :width].astype(stacked.dtype)

        return emit

    def forward(y, carry):
        here = row_at(y, width)
        pre = jnp.dot(ahead[0], stacked[: 3 * channels, here], preferred_element_type=jnp.float32)
        for tap_row in (1, 2):
            pre = pre + jnp.dot(
                ahead[tap_row], stacked[: 3 * channels, row_at(y + tap_row, width)], preferred_element_type=jnp.float32
            )
        gate = jax.nn.sigmoid(pre)
        hidden = (pre * gate).astype(jnp.bfloat16)
        hidden_all[:, here] = hidden
        steep[:, here] = gate * (1.0 + pre * (1.0 - gate))
        logit = jnp.dot(class_in[...], hidden, preferred_element_type=jnp.float32)
        chance[:, here] = jax.nn.sigmoid(logit)
        return carry

    for sweep in range(ITERS):
        now = probs if sweep == 0 else sweeps.at[sweep - 1]
        later = refined if sweep == ITERS - 1 else sweeps.at[sweep]
        finish_sides(copies)
        spread(now, prob_rows.at[sweep], prob_rims.at[sweep], rows, width, REACH, emit_probs, rows)

        def gather(y, carry):
            running = weights[0, :, row_at(y, width)] * moved_now[0, :, row_at(y + REACH, width)]
            for index, (off_y, off_x) in enumerate(tap_list()):
                running = running + (
                    weights[index + 1, :, row_at(y, width)]
                    * moved_now[SHIFTS.index(off_x), :, row_at(y + REACH + off_y, width)]
                )
            later[:, row_at(y, width)] = running
            return carry

        lax.fori_loop(0, rows, gather, 0, unroll=2)
        if sweep < ITERS - 1:
            pack_sides(later, packs.at[sweep + 1], rows, width, REACH, rows)
            copies = side_copies(
                later, packs.at[sweep + 1], prob_rows.at[sweep + 1], prob_rims.at[sweep + 1], sems, 16 + 8 * sweep, span
            )
            start_sides(copies)
            if sweep == 0:
                finish_sides(cell_copies)
                unturn_rims(cell_rims, wide_rims)
                spread(cells, cell_rows, wide_rims, rows, width, 1, stack_into(channels))
            elif sweep < ITERS - 2:
                lax.fori_loop(0, rows // 2, forward, 0, unroll=2)
            else:
                lax.fori_loop(rows // 2, rows, forward, 0, unroll=2)

    class_part[...] = jnp.zeros_like(class_part)

    def backward(y, carry):
        here = row_at(y, width)
        wrong = (chance[:, here] - refined[:, here]).astype(jnp.bfloat16)
        slope = jnp.dot(class_out[...], wrong, preferred_element_type=jnp.float32) * steep[:, here]
        error[:, here] = slope.astype(jnp.bfloat16)
        error_turned[here, :] = slope.T.astype(jnp.bfloat16)
        class_part[...] += lax.dot_general(
            wrong, hidden_all[:, here], (((1,), (1,)), ((), ())), preferred_element_type=jnp.float32
        )
        return carry

    lax.fori_loop(0, rows, backward, 0, unroll=2)

    def run_chunk(chunk):
        for index in range(3):
            parts[chunk, index * channels : (index + 1) * channels, :] = jnp.dot(
                stacked[index * channels : (index + 1) * channels, chunk * width : chunk * width + pixels],
                error_turned[...],
                preferred_element_type=jnp.float32,
            )
        if parts.shape[1] > 3 * channels:
            parts[chunk, 3 * channels :, :] = jnp.zeros((parts.shape[1] - 3 * channels, parts.shape[2]), jnp.float32)

    def features(y, carry):
        total = jnp.dot(back[0], stacked[: 3 * hidden_size, row_at(y, width)], preferred_element_type=jnp.float32)
        for tap_row in (1, 2):
            total = total + jnp.dot(
                back[tap_row], stacked[: 3 * hidden_size, row_at(y + tap_row, width)], preferred_element_type=jnp.float32
            )
        slope_grad[:, row_at(y, width)] = total.astype(jnp.bfloat16)
        return carry

    def chunk_phases(chunk):
        extra = (class_part, class_grad, cls_core, cls_row, cls_z) if chunk == 0 else None
        return reduce_body(
            nr, nz, scale, parts.at[chunk], conv_out.at[chunk], core_buf.at[chunk], row_buf.at[chunk],
            z_buf.at[chunk], fin.at[chunk], reduce_sems.at[chunk], extra,
        )

    phases = [chunk_phases(chunk) for chunk in range(3)]
    pack_sides(error, wide_packs, rows, width, 1)
    turn_packs(wide_packs, error_packs)
    copies = side_copies(error, error_packs, error_rows, error_rims, sems, base + 8, width)
    start_sides(copies)
    run_chunk(0)
    next(phases[0])
    run_chunk(1)
    next(phases[0])
    next(phases[1])
    run_chunk(2)
    next(phases[1])
    next(phases[2])
    finish_sides(copies)
    unturn_rims(error_rims, wide_rims)
    spread(error, error_rows, wide_rims, rows, width, 1, stack_into(hidden_size))
    turn = 0
    while phases:
        phases = [phase for phase in phases if next(phase, True) is None]
        if turn < 4:
            lax.fori_loop(turn * rows // 4, (turn + 1) * rows // 4, features, 0, unroll=2)
        turn += 1


def whole_step(feats, probs, cells, conv_weight, class_weight, rows, width):
    teacher_channels = feats.shape[0]
    channels, pixels = cells.shape
    hidden, classes = class_weight.shape
    nr = lax.axis_size("row")
    nz = lax.axis_size("col") // 2
    unit = nr * nz * 16
    span = REACH * width
    wide = (rows + 2) * width
    wider = (rows + 2 * REACH) * width
    total = -(-3 * channels // unit) * unit
    turned = -(-rows // 16) * 16
    f32, bf16 = jnp.float32, jnp.bfloat16
    out = pl.pallas_call(
        functools.partial(step_kernel, nr, nz, rows, width, 1.0 / pixels),
        out_shape=(
            jax.ShapeDtypeStruct((classes, pixels), f32),
            jax.ShapeDtypeStruct((channels, pixels), bf16),
            jax.ShapeDtypeStruct((3, total, hidden), f32),
            jax.ShapeDtypeStruct((classes, hidden), f32),
        ),
        in_specs=[pl.BlockSpec(memory_space=pltpu.VMEM)] * 5,
        out_specs=[pl.BlockSpec(memory_space=pltpu.VMEM)] * 4,
        scratch_shapes=[
            pltpu.VMEM((3, hidden, 3 * channels), bf16),
            pltpu.VMEM((3, channels, 3 * hidden), bf16),
            pltpu.VMEM((hidden, classes), bf16),
            pltpu.VMEM((2, max(channels, hidden), 128), f32),
            pltpu.VMEM((6, max(channels, hidden), 128), f32),
            pltpu.VMEM((len(SHIFTS), teacher_channels, wider), f32),
            pltpu.VMEM((25, 8, pixels), f32),
            pltpu.VMEM((ITERS - 1, classes, pixels), f32),
            pltpu.VMEM((len(SHIFTS), classes, wider), f32),
            pltpu.VMEM((2, teacher_channels, 128), bf16),
            pltpu.VMEM((2, teacher_channels, span), bf16),
            pltpu.VMEM((6, teacher_channels, 128), bf16),
            pltpu.VMEM((ITERS, 2, classes, 128), f32),
            pltpu.VMEM((ITERS, 2, classes, span), f32),
            pltpu.VMEM((ITERS, 6, classes, 128), f32),
            pltpu.VMEM((3 * max(channels, hidden), wide), bf16),
            pltpu.VMEM((hidden, pixels), f32),
            pltpu.VMEM((hidden, pixels), bf16),
            pltpu.VMEM((classes, pixels), f32),
            pltpu.VMEM((hidden, pixels), bf16),
            pltpu.VMEM((pixels, hidden), bf16),
            pltpu.VMEM((3, total, hidden), f32),
            pltpu.VMEM((classes, hidden), f32),
            pltpu.VMEM((2, turned, channels), bf16),
            pltpu.VMEM((2, channels, width), bf16),
            pltpu.VMEM((6, turned, channels), bf16),
            pltpu.VMEM((2, turned, hidden), bf16),
            pltpu.VMEM((2, hidden, width), bf16),
            pltpu.VMEM((6, turned, hidden), bf16),
            pltpu.SemaphoreType.DMA((2, 24 + 8 * ITERS)),
        ]
        + reduce_scratch(nr, nz, total, classes, hidden),
        compiler_params=pltpu.CompilerParams(collective_id=0, has_side_effects=True, vmem_limit_bytes=60 * 2**20),
    )(feats, probs, cells, conv_weight, class_weight.T)
    return out[0], out[1], out[2][:, : 3 * channels], out[3]


def shards(teacher_feats, teacher_probs, student_feats, conv_weight, class_weight):
    classes, rows, width = teacher_probs.shape
    channels = student_feats.shape[0]
    pixels = rows * width
    refined, feature_grad, grad_conv, grad_class = whole_step(
        teacher_feats.reshape(teacher_feats.shape[0], pixels),
        teacher_probs.reshape(classes, pixels),
        student_feats.reshape(channels, pixels),
        conv_weight,
        class_weight,
        rows,
        width,
    )
    return (
        refined.reshape(classes, rows, width),
        feature_grad.reshape(channels, rows, width),
        grad_conv.reshape(conv_weight.shape),
        grad_class.T,
    )


def solution(mesh):
    in_specs = (P(None, "row", "col"), P(None, "row", "col"), P(None, "row", "col"), P(), P())
    out_specs = (P(None, "row", "col"), P(None, "row", "col"), P(), P())
    return jax.shard_map(shards, mesh=mesh, in_specs=in_specs, out_specs=out_specs, check_vma=False)
```
